128 devices in a mesh: gx: 4 (over y), gy: 32 (over z, x, core).
Axes of the slice: x: 4, y: 4, z: 4, core: 2. Of those that a mesh axis runs over, the one named last changes fastest.
Arguments:
- cam_pose: float32 [7, 32768], P(None, ('gx', 'gy')), may hold values from -0.5 to 2, as said below
- points: float32 [3, 524288], P(None, ('gx', 'gy')), may hold values from -1.5 to 8, as said below
- obs_uv: float32 [2, 128, 128, 128], P(None, ('gx', 'gy')), may hold values from -0.6 to 0.6
- obs_cam: int32 [128, 128, 128], P(('gx', 'gy')), may hold values from 0 to 255
- obs_pt: int32 [128, 128, 128], P(('gx', 'gy')), may hold values from 0 to 4095
- block_count: int32 [128, 128], P(('gx', 'gy')), may hold values from 1 to 128, as said below
- send_list: int32 [128, 128, 16], P(('gx', 'gy')), may hold values from 0 to 255
- edge_slot: int32 [8, 32768], P(None, ('gx', 'gy')), may hold values from 0 to 2047
- edge_weight: float32 [8, 32768], P(None, ('gx', 'gy')), may hold values from 0.2 to 1
Outputs:
- cam_step: float32 [6, 32768], P(None, ('gx', 'gy'))
- cam_residual: float32 [6, 32768], P(None, ('gx', 'gy'))
The draws below stay inside these ranges and needn't reach their ends.
Inputs may be any that keep to these rules, and one draw needn't show every extreme that they name: `cam_pose`: rows 0 in [0.9, 1.1], rows 1 to 3 in [-0.15, 0.15], rows 4 and 5 in [-0.5, 0.5], row 6 in [1, 2]. `points`: rows 0 and 1 in [-1.5, 1.5], row 2 in [4, 8]. Slot j of block [d, s] is live exactly when j < block_count[d, s]; some blocks are full.
All inputs are finite; a program needn't handle non-finite values.
Results may differ from the reference program's by a relative error of at most 0.00021.
Values sent between devices are 32-bit elements; how exact they have to be, the bound alone decides.
No kernel may reach another device: no remote copies, remote signals or barrier semaphores. Data moves between devices by JAX's collectives and lax.ppermute only.
A program may use at most 64 MiB of HBM per device.

```python
import math
import jax
import jax.numpy as jnp

SLOT = 128
CSLOT = 16
NEIGHBORS = 8
ITERS = 2
CAM_DEV = 256
PT_DEV = 4096
CAMS = 32768
PTS = 524288
N_GX = 4
N_GY = 32


def draw_cam_pose(key, part):
    keys = jax.random.split(key, 4)
    lead = jax.random.uniform(keys[0], (1, CAMS), jnp.float32, 0.9, 1.1)
    vector_part = jax.random.uniform(keys[1], (3, CAMS), jnp.float32, -0.15, 0.15)
    shift = jax.random.uniform(keys[2], (2, CAMS), jnp.float32, -0.5, 0.5)
    height = jax.random.uniform(keys[3], (1, CAMS), jnp.float32, 1.0, 2.0)
    return jnp.concatenate([lead, vector_part, shift, height], 0)


def draw_points(key, part):
    keys = jax.random.split(key, 2)
    planar = jax.random.uniform(keys[0], (2, PTS), jnp.float32, -1.5, 1.5)
    height = jax.random.uniform(keys[1], (1, PTS), jnp.float32, 4.0, 8.0)
    return jnp.concatenate([planar, height], 0)


def draw_block_count(key, part):
    devices = N_GX * N_GY
    keys = jax.random.split(key, 4)
    heavy = jax.random.randint(keys[0], (devices,), 0, 8) == 0
    forced = jax.random.randint(keys[1], (), 0, devices)
    heavy = heavy | (jnp.arange(devices) == forced)
    lowest = max(SLOT // 4, 1)
    capacity = jnp.where(heavy, SLOT, max(2 * SLOT // 3, lowest)).astype(jnp.int32)
    counts = jax.random.randint(keys[2], (devices, devices), lowest, capacity[:, None] + 1)
    full_source = jax.random.randint(keys[3], (devices,), 0, devices)
    filled = heavy[:, None] & (jnp.arange(devices)[None, :] == full_source[:, None])
    return jnp.where(filled, SLOT, counts).astype(jnp.int32)


def set_ends(array, rng, low, largest):
    spot = [jax.random.randint(jax.random.fold_in(rng, axis), (), 0, length) for axis, length in enumerate(array.shape)]
    widest = array.shape.index(max(array.shape))
    beside = spot[:widest] + [(spot[widest] + 1) % array.shape[widest]] + spot[widest + 1:]
    return array.at[tuple(spot)].set(low).at[tuple(beside)].set(largest)


def block_levels(rng, shape, cuts, smallest, largest):
    loudness, own = 1.0, jax.random.fold_in(rng, 6)
    for dim, parts in cuts:
        steps = jnp.exp(jax.random.uniform(jax.random.fold_in(own, dim), (parts,), jnp.float32, smallest / len(cuts), largest / len(cuts)))
        loudness = loudness * jnp.repeat(steps, shape[dim] // parts).reshape([-1 if axis == dim else 1 for axis in range(len(shape))])
    return loudness


def setup_inputs(seed: int = 0) -> dict:
    key_of = jax.random.split(jax.random.key(seed), 10)
    return {
        "cam_pose": draw_cam_pose(jax.random.fold_in(key_of[9], 71), 0),
        "points": draw_points(jax.random.fold_in(key_of[9], 71), 0),
        "obs_uv": jnp.clip(jax.random.uniform(key_of[2], (2, N_GX * N_GY, N_GX * N_GY, SLOT), jnp.float32, -0.6, 0.6) * block_levels(key_of[2], (2, N_GX * N_GY, N_GX * N_GY, SLOT), ((1, 128),), -0.4, 0.0), -0.6, 0.6),
        "obs_cam": set_ends(jax.random.randint(key_of[3], (N_GX * N_GY, N_GX * N_GY, SLOT), 0, CAM_DEV), jax.random.fold_in(key_of[3], 1), 0, CAM_DEV - 1).astype(jnp.int32),
        "obs_pt": set_ends(jax.random.randint(key_of[4], (N_GX * N_GY, N_GX * N_GY, SLOT), 0, PT_DEV), jax.random.fold_in(key_of[4], 1), 0, PT_DEV - 1).astype(jnp.int32),
        "block_count": draw_block_count(jax.random.fold_in(key_of[9], 71), 0),
        "send_list": set_ends(jax.random.randint(key_of[6], (N_GX * N_GY, N_GX * N_GY, CSLOT), 0, CAM_DEV), jax.random.fold_in(key_of[6], 1), 0, CAM_DEV - 1).astype(jnp.int32),
        "edge_slot": set_ends(jax.random.randint(key_of[7], (NEIGHBORS, CAMS), 0, N_GX * N_GY * CSLOT), jax.random.fold_in(key_of[7], 1), 0, (N_GX * N_GY * CSLOT) - 1).astype(jnp.int32),
        "edge_weight": jnp.clip(jnp.exp(math.log(1.0) - 1.609438 * jax.random.uniform(key_of[8], (NEIGHBORS, CAMS), jnp.float32) ** block_levels(key_of[8], (NEIGHBORS, CAMS), ((1, 128),), -0.2, 0.2)), 0.2, 1.0),
    }


DAMPING = 1.0
SYMMETRIC_PAIRS = [(a, b) for a in range(6) for b in range(a, 6)]
POINT_PAIRS = [(0, 0), (0, 1), (0, 2), (1, 1), (1, 2), (2, 2)]


def rotation(quaternion):
    q0, q1, q2, q3 = quaternion[0], quaternion[1], quaternion[2], quaternion[3]
    inverse_norm = 1.0 / (q0 * q0 + q1 * q1 + q2 * q2 + q3 * q3)
    entries = [q0 * q0 + q1 * q1 - q2 * q2 - q3 * q3, 2.0 * (q1 * q2 - q0 * q3), 2.0 * (q1 * q3 + q0 * q2),
               2.0 * (q1 * q2 + q0 * q3), q0 * q0 - q1 * q1 + q2 * q2 - q3 * q3, 2.0 * (q2 * q3 - q0 * q1),
               2.0 * (q1 * q3 - q0 * q2), 2.0 * (q2 * q3 + q0 * q1), q0 * q0 - q1 * q1 - q2 * q2 + q3 * q3]
    return jnp.stack([value * inverse_norm for value in entries])


def eliminate(measured, rot_rows, translation, point_rows, live_mask, point_index, count_points):
    cam_pt = [rot_rows[3 * a] * point_rows[0] + rot_rows[3 * a + 1] * point_rows[1] + rot_rows[3 * a + 2] * point_rows[2] + translation[a] for a in range(3)]
    inv_depth = 1.0 / cam_pt[2]
    proj_u = cam_pt[0] * inv_depth
    proj_v = cam_pt[1] * inv_depth
    residue = [(proj_u - measured[0]) * live_mask, (proj_v - measured[1]) * live_mask]
    scaled = inv_depth * live_mask
    zeros_row = jnp.zeros_like(scaled)
    jac_proj = [[scaled, zeros_row, -proj_u * scaled], [zeros_row, scaled, -proj_v * scaled]]
    cross_matrix = [[zeros_row, cam_pt[2], -cam_pt[1]], [-cam_pt[2], zeros_row, cam_pt[0]], [cam_pt[1], -cam_pt[0], zeros_row]]
    jac_cam = []
    jac_point = []
    for i in range(2):
        jac_row = [jac_proj[i][0] * cross_matrix[0][k] + jac_proj[i][1] * cross_matrix[1][k] + jac_proj[i][2] * cross_matrix[2][k] for k in range(3)]
        jac_cam.append(jac_row + jac_proj[i])
        jac_point.append([jac_proj[i][0] * rot_rows[k] + jac_proj[i][1] * rot_rows[3 + k] + jac_proj[i][2] * rot_rows[6 + k] for k in range(3)])
    point_terms = [jac_point[0][k] * jac_point[0][l] + jac_point[1][k] * jac_point[1][l] for (k, l) in POINT_PAIRS]
    point_terms = point_terms + [jac_point[0][k] * residue[0] + jac_point[1][k] * residue[1] for k in range(3)]
    point_sums = jnp.zeros((9, count_points), jnp.float32).at[:, point_index].add(jnp.stack(point_terms))
    hess = [point_sums[0] + DAMPING, point_sums[1], point_sums[2], point_sums[3] + DAMPING, point_sums[4], point_sums[5] + DAMPING]
    cofactor = [hess[3] * hess[5] - hess[4] * hess[4], hess[2] * hess[4] - hess[1] * hess[5], hess[1] * hess[4] - hess[2] * hess[3],
                hess[0] * hess[5] - hess[2] * hess[2], hess[1] * hess[2] - hess[0] * hess[4], hess[0] * hess[3] - hess[1] * hess[1]]
    determinant = hess[0] * cofactor[0] + hess[1] * cofactor[1] + hess[2] * cofactor[2]
    per_point = jnp.stack([value / determinant for value in cofactor] + [point_sums[6], point_sums[7], point_sums[8]])[:, point_index]
    inv_full = [[per_point[0], per_point[1], per_point[2]], [per_point[1], per_point[3], per_point[4]], [per_point[2], per_point[4], per_point[5]]]
    grad_point = [per_point[6], per_point[7], per_point[8]]
    coupling = [[jac_cam[0][a] * jac_point[0][k] + jac_cam[1][a] * jac_point[1][k] for k in range(3)] for a in range(6)]
    coupled = [[coupling[a][0] * inv_full[0][k] + coupling[a][1] * inv_full[1][k] + coupling[a][2] * inv_full[2][k] for k in range(3)] for a in range(6)]
    schur_block = [jac_cam[0][a] * jac_cam[0][b] + jac_cam[1][a] * jac_cam[1][b] - (coupled[a][0] * coupling[b][0] + coupled[a][1] * coupling[b][1] + coupled[a][2] * coupling[b][2]) for (a, b) in SYMMETRIC_PAIRS]
    reduced = [jac_cam[0][a] * residue[0] + jac_cam[1][a] * residue[1] - (coupled[a][0] * grad_point[0] + coupled[a][1] * grad_point[1] + coupled[a][2] * grad_point[2]) for a in range(6)]
    return jnp.stack(schur_block + reduced)


def block_product(blocks, vector):
    lookup = {}
    for index, (a, b) in enumerate(SYMMETRIC_PAIRS):
        lookup[(a, b)] = index
        lookup[(b, a)] = index
    return jnp.stack([sum(blocks[lookup[(a, b)]] * vector[b] for b in range(6)) for a in range(6)])


def reference(cam_pose, points, obs_uv, obs_cam, obs_pt, block_count, send_list, edge_slot, edge_weight):
    devices = N_GX * N_GY
    shape = (devices, devices, SLOT)
    source = jax.lax.broadcasted_iota(jnp.int32, shape, 0)
    target = jax.lax.broadcasted_iota(jnp.int32, shape, 1)
    position = jax.lax.broadcasted_iota(jnp.int32, shape, 2)
    cam_global = (source * CAM_DEV + obs_cam).reshape(-1)
    pt_global = (target * PT_DEV + jnp.transpose(obs_pt, (1, 0, 2))).reshape(-1)
    live_mask = (position < jnp.transpose(block_count)[:, :, None]).astype(jnp.float32).reshape(-1)
    rot_rows = rotation(cam_pose[0:4])[:, cam_global]
    translation = cam_pose[4:7][:, cam_global]
    measured = obs_uv.reshape(2, -1)
    entries = eliminate(measured, rot_rows, translation, points[:, pt_global], live_mask, pt_global, PTS)
    camera_sums = jnp.zeros((27, CAMS), jnp.float32).at[:, cam_global].add(entries)
    blocks = camera_sums[0:21]
    gradient = camera_sums[21:27]
    owner_device = (jnp.arange(CAMS) // CAM_DEV).astype(jnp.int32)
    from_device = (edge_slot // CSLOT).astype(jnp.int32)
    neighbour = from_device * CAM_DEV + send_list[from_device, owner_device[None, :], edge_slot % CSLOT]
    flat_neighbour = neighbour.reshape(-1)

    def apply_system(vector):
        edge_term = edge_weight[None] * (vector[:, None, :] - vector[:, neighbour])
        applied = block_product(blocks, vector) + DAMPING * vector + jnp.sum(edge_term, axis=1)
        return applied.at[:, flat_neighbour].add(-edge_term.reshape(6, -1))

    diagonal_entries = jnp.stack([blocks[SYMMETRIC_PAIRS.index((a, a))] for a in range(6)]) + DAMPING
    update_step = jnp.zeros((6, CAMS), jnp.float32)
    residual = -gradient
    precond = residual / diagonal_entries
    direction = precond
    precond_dot = jnp.sum(residual * precond)
    for iteration in range(ITERS):
        product_image = apply_system(direction)
        step_size = precond_dot / jnp.sum(direction * product_image)
        update_step = update_step + step_size * direction
        residual = residual - step_size * product_image
        if iteration + 1 < ITERS:
            precond = residual / diagonal_entries
            next_dot = jnp.sum(residual * precond)
            direction = precond + (next_dot / precond_dot) * direction
            precond_dot = next_dot
    return update_step, residual
```

```python
import functools

import jax
import jax.numpy as jnp
from jax import lax
from jax.experimental import pallas as pl
from jax.experimental.pallas import tpu as pltpu
from jax.sharding import PartitionSpec as P

AXES = ("gx", "gy")
DAMPING = 1.0
SYMMETRIC_PAIRS = [(a, b) for a in range(6) for b in range(a, 6)]
LOOKUP = {}
for _place, (_a, _b) in enumerate(SYMMETRIC_PAIRS):
    LOOKUP[_a, _b] = _place
    LOOKUP[_b, _a] = _place
POINT_PAIRS = [(0, 0), (0, 1), (0, 2), (1, 1), (1, 2), (2, 2)]
PARTS = 3

F32 = jnp.float32
BF16 = jnp.bfloat16


def call(kernel, name, out_shape, scratch=(), flops=1_000_000, bytes_accessed=1_000_000):
    return pl.pallas_call(
        kernel,
        out_shape=out_shape,
        scratch_shapes=list(scratch),
        name=name,
        compiler_params=pltpu.CompilerParams(vmem_limit_bytes=48 * 1024 * 1024),
        cost_estimate=pl.CostEstimate(
            flops=flops, bytes_accessed=bytes_accessed, transcendentals=0
        ),
    )


def array(*shape):
    return jax.ShapeDtypeStruct(shape, F32)


def take(table, index):
    return jnp.take_along_axis(table, index, axis=1, mode="promise_in_bounds")


def spread(row, count):
    return jnp.broadcast_to(row, (count, row.shape[1]))


def parts_of(value):
    parts = []
    for _ in range(PARTS):
        part = value.astype(BF16).astype(F32)
        value = value - part
        parts.append(part)
    return parts


def dot_lanes(left, right):
    return lax.dot_general(left, right, (((1,), (1,)), ((), ())), preferred_element_type=F32)


def total(value):
    return jnp.sum(jnp.sum(value, axis=1, keepdims=True), axis=0, keepdims=True)


def pose_kernel(pose_ref, cam_ref, uv_ref, out_ref, table_ref):
    inverse = 1.0 / pose_ref[0:1, :]
    table_ref[0:3, :] = pose_ref[1:4, :] * inverse
    table_ref[3:6, :] = pose_ref[4:7, :]
    table_ref[6:8, :] = jnp.zeros((2, 256), F32)
    low, high = table_ref[:, 0:128], table_ref[:, 128:256]

    def tile(t, carry):
        base = pl.multiple_of(t * 8, 8)
        index = cam_ref[pl.ds(base, 8), :]
        lane = index & 127
        for i in range(8):
            where = spread(lane[i : i + 1, :], 8)
            upper = spread(index[i : i + 1, :], 8) >= 128
            out_ref[pl.ds(pl.multiple_of(base * 8 + 8 * i, 8), 8), :] = jnp.where(
                upper, take(high, where), take(low, where)
            )
        out_ref[pl.ds(base * 8 + 6, 8, stride=8), :] = uv_ref[0, pl.ds(base, 8), :]
        out_ref[pl.ds(base * 8 + 7, 8, stride=8), :] = uv_ref[1, pl.ds(base, 8), :]
        return carry

    lax.fori_loop(0, 16, tile, 0)


def position_kernel(points_ref, index_ref, out_ref):
    def group(g, carry):
        base = pl.multiple_of(g * 32, 32)
        index = [index_ref[pl.ds(base + 8 * k, 8), :] for k in range(4)]
        lane = [value & 127 for value in index]
        chunk = [value >> 7 for value in index]
        found = [[jnp.zeros((8, 128), F32) for _ in range(4)] for _ in range(3)]
        for h in range(32):
            for r in range(3):
                row = spread(points_ref[r : r + 1, h * 128 : (h + 1) * 128], 8)
                for k in range(4):
                    found[r][k] = jnp.where(chunk[k] == h, take(row, lane[k]), found[r][k])
        for r in range(3):
            for k in range(4):
                out_ref[r, pl.ds(base + 8 * k, 8), :] = found[r][k]
        return carry

    lax.fori_loop(0, 4, group, 0)


def onehot_rows(rows_ref, row, count, where, iota):
    value = spread(row, 16).astype(BF16)
    one, zero = jnp.ones((), BF16), jnp.zeros((), BF16)
    for q in range(count // 16):
        rows_ref[q * 16 : (q + 1) * 16, where : where + 128] = jnp.where(
            iota[q * 16 : (q + 1) * 16] == value, one, zero
        )


def iota_bf16(count):
    return lax.broadcasted_iota(jnp.int32, (count, 128), 0).astype(F32).astype(BF16)


def eliminate_kernel(
    recv_ref, position_ref, index_ref, count_ref, out_ref, term_ref, keep_ref, left_ref, hot_ref,
    sum_ref, table_ref,
):
    live_count = jnp.transpose(spread(count_ref[0:1, :], 128))
    keep_ref[11, :, :] = jnp.where(
        lax.broadcasted_iota(jnp.int32, (128, 128), 1) < live_count, 1.0, 0.0
    )

    def prepare(t, carry):
        base = pl.multiple_of(t * 8, 8)
        row = [recv_ref[pl.ds(base * 8 + r, 8, stride=8), :] for r in range(8)]
        x = [position_ref[r, pl.ds(base, 8), :] for r in range(3)]
        live = keep_ref[11, pl.ds(base, 8), :]
        q1, q2, q3 = row[0], row[1], row[2]
        s1, s2, s3 = q1 * q1, q2 * q2, q3 * q3
        scale = 1.0 / (1.0 + s1 + s2 + s3)
        q12, q13, q23 = q1 * q2, q1 * q3, q2 * q3
        rot = [
            (1.0 + s1 - s2 - s3) * scale,
            2.0 * (q12 - q3) * scale,
            2.0 * (q13 + q2) * scale,
            2.0 * (q12 + q3) * scale,
            (1.0 - s1 + s2 - s3) * scale,
            2.0 * (q23 - q1) * scale,
            2.0 * (q13 - q2) * scale,
            2.0 * (q23 + q1) * scale,
            (1.0 - s1 - s2 + s3) * scale,
        ]
        cam = [
            rot[3 * a] * x[0] + rot[3 * a + 1] * x[1] + rot[3 * a + 2] * x[2] + row[3 + a]
            for a in range(3)
        ]
        inverse = 1.0 / cam[2]
        u, v = cam[0] * inverse, cam[1] * inverse
        residue = [(u - row[6]) * live, (v - row[7]) * live]
        scaled = inverse * live
        jac = [
            [scaled * (rot[k] - u * rot[6 + k]) for k in range(3)],
            [scaled * (rot[3 + k] - v * rot[6 + k]) for k in range(3)],
        ]
        terms = [jac[0][k] * jac[0][l] + jac[1][k] * jac[1][l] for k, l in POINT_PAIRS]
        terms += [jac[0][k] * residue[0] + jac[1][k] * residue[1] for k in range(3)]
        for r in range(9):
            term_ref[r, pl.ds(base, 8), :] = terms[r]
        for r, value in enumerate(jac[0] + jac[1] + residue + [u, v, inverse]):
            keep_ref[r, pl.ds(base, 8), :] = value
        return carry

    lax.fori_loop(0, 16, prepare, 0)

    iota_chunk, iota_lane = iota_bf16(16), iota_bf16(256)
    zero = jnp.zeros((), BF16)
    sum_ref[...] = jnp.zeros_like(sum_ref)

    def build(t, side):
        base = pl.multiple_of(t * 8, 8)
        index = index_ref[pl.ds(base, 8), :]
        lane, chunk = (index & 255).astype(F32), (index >> 8).astype(F32)
        masks = []
        for i in range(8):
            onehot_rows(hot_ref.at[side], lane[i : i + 1, :], 256, i * 128, iota_lane)
            masks.append(iota_chunk == spread(chunk[i : i + 1, :], 16).astype(BF16))
        for r in range(9):
            for n, part in enumerate(parts_of(term_ref[r, pl.ds(base, 8), :])):
                at = (n * 9 + r) * 16
                for i in range(8):
                    left_ref[side, at : at + 16, i * 128 : (i + 1) * 128] = jnp.where(
                        masks[i], spread(part[i : i + 1, :], 16).astype(BF16), zero
                    )

    def product(side):
        sum_ref[...] += dot_lanes(left_ref[side], hot_ref[side])

    build(0, 0)

    def pair(t, carry):
        build(2 * t + 1, 1)
        product(0)
        build(jnp.minimum(2 * t + 2, 15), 0)
        product(1)
        return carry

    lax.fori_loop(0, 8, pair, 0)

    sums = []
    for r in range(9):
        value = sum_ref[r * 16 : (r + 1) * 16, :]
        for n in range(1, PARTS):
            value = value + sum_ref[(n * 9 + r) * 16 : (n * 9 + r + 1) * 16, :]
        sums.append(value)
    hess = [sums[0] + DAMPING, sums[1], sums[2], sums[3] + DAMPING, sums[4], sums[5] + DAMPING]
    cofactor = [
        hess[3] * hess[5] - hess[4] * hess[4],
        hess[2] * hess[4] - hess[1] * hess[5],
        hess[1] * hess[4] - hess[2] * hess[3],
        hess[0] * hess[5] - hess[2] * hess[2],
        hess[1] * hess[2] - hess[0] * hess[4],
        hess[0] * hess[3] - hess[1] * hess[1],
    ]
    determinant = hess[0] * cofactor[0] + hess[1] * cofactor[1] + hess[2] * cofactor[2]
    inv = [value / determinant for value in cofactor]
    grad = sums[6:9]
    solved = [
        inv[0] * grad[0] + inv[1] * grad[1] + inv[2] * grad[2],
        inv[1] * grad[0] + inv[3] * grad[1] + inv[4] * grad[2],
        inv[2] * grad[0] + inv[4] * grad[1] + inv[5] * grad[2],
    ]
    for r, value in enumerate(inv + solved):
        table_ref[r * 16 : (r + 1) * 16, :] = value

    def group(g, carry):
        base = pl.multiple_of(g * 16, 16)
        index = [index_ref[pl.ds(base + 8 * k, 8), :] for k in range(2)]
        lane = [value & 127 for value in index]
        chunk = [value >> 7 for value in index]
        found = [[jnp.zeros((8, 128), F32) for _ in range(9)] for _ in range(2)]
        for h in range(32):
            half = (h % 2) * 128
            for r in range(9):
                at = r * 16 + h // 2
                row = spread(table_ref[at : at + 1, half : half + 128], 8)
                for k in range(2):
                    found[k][r] = jnp.where(chunk[k] == h, take(row, lane[k]), found[k][r])
        for k in range(2):
            here = pl.multiple_of(base + 8 * k, 8)
            kept = [keep_ref[r, pl.ds(here, 8), :] for r in range(12)]
            i0, i1, i2, i3, i4, i5, g0, g1, g2 = found[k]
            p, q = kept[0:3], kept[3:6]
            pv = [
                i0 * p[0] + i1 * p[1] + i2 * p[2],
                i1 * p[0] + i3 * p[1] + i4 * p[2],
                i2 * p[0] + i4 * p[1] + i5 * p[2],
            ]
            qv = [
                i0 * q[0] + i1 * q[1] + i2 * q[2],
                i1 * q[0] + i3 * q[1] + i4 * q[2],
                i2 * q[0] + i4 * q[1] + i5 * q[2],
            ]
            live = kept[11]
            values = [
                kept[8],
                kept[9],
                kept[10],
                live - (pv[0] * p[0] + pv[1] * p[1] + pv[2] * p[2]),
                -(pv[0] * q[0] + pv[1] * q[1] + pv[2] * q[2]),
                live - (qv[0] * q[0] + qv[1] * q[1] + qv[2] * q[2]),
                kept[6] - (p[0] * g0 + p[1] * g1 + p[2] * g2),
                kept[7] - (q[0] * g0 + q[1] * g1 + q[2] * g2),
            ]
            for r, value in enumerate(values):
                out_ref[pl.ds(here * 8 + r, 8, stride=8), :] = value
        return carry

    lax.fori_loop(0, 8, group, 0)


def exchange_out(vector_ref, slots_ref, edge_ref, weight_ref, out_ref, turn_ref, left_ref, hot_ref):
    low, high = vector_ref[:, 0:128], vector_ref[:, 128:256]
    for j in range(16):
        index = spread(slots_ref[j : j + 1, :], 8)
        lane = index & 127
        turn_ref[8 * j : 8 * j + 8, :] = jnp.where(index >= 128, take(high, lane), take(low, lane))
    out_ref[:, 0:128] = jnp.transpose(turn_ref[...])
    iota = iota_bf16(128)
    for k in range(8):
        for h in range(2):
            where = (2 * k + h) * 128
            edge = edge_ref[k : k + 1, h * 128 : (h + 1) * 128]
            onehot_rows(hot_ref, (edge >> 4).astype(F32), 128, where, iota)
            slot = spread(edge & 15, 8)
            weight = spread(weight_ref[k : k + 1, h * 128 : (h + 1) * 128], 8)
            for n, part in enumerate(parts_of(weight * (low, high)[h])):
                for j in range(0, 16, 2):
                    both = jnp.concatenate(
                        [jnp.where(slot == j, part, 0.0), jnp.where(slot == j + 1, part, 0.0)], 0
                    )
                    left_ref[n, 8 * j : 8 * j + 16, where : where + 128] = both.astype(BF16)
    summed = dot_lanes(hot_ref[...], left_ref[0])
    for n in range(1, PARTS):
        summed = summed + dot_lanes(hot_ref[...], left_ref[n])
    out_ref[:, 128:256] = summed


def exchange_in(recv_ref, slots_ref, edge_ref, weight_ref, turn_ref, few_ref, cams_ref, near_ref):
    turn_ref[...] = jnp.transpose(recv_ref[:, 0:128])
    for h in range(2):
        sums = jnp.zeros((8, 128), F32)
        for k in range(8):
            edge = edge_ref[k : k + 1, h * 128 : (h + 1) * 128]
            slot, peer = spread(edge & 15, 8), spread(edge >> 4, 8)
            near = jnp.zeros((8, 128), F32)
            for j in range(16):
                near = jnp.where(slot == j, take(turn_ref[8 * j : 8 * j + 8, :], peer), near)
            sums = sums + spread(weight_ref[k : k + 1, h * 128 : (h + 1) * 128], 8) * near
        near_ref[:, h * 128 : (h + 1) * 128] = sums
    scalar = jnp.sum(turn_ref[7:8, :], axis=1, keepdims=True)
    turn_ref[...] = jnp.transpose(recv_ref[:, 128:256])
    iota = iota_bf16(256)
    for j in range(16):
        parts = parts_of(turn_ref[8 * j : 8 * j + 8, :])
        parts += [jnp.zeros((8, 128), F32)] * (4 - PARTS)
        few_ref[:, j * 128 : (j + 1) * 128] = jnp.concatenate(parts, 0).astype(BF16)
        onehot_rows(cams_ref, slots_ref[j : j + 1, :].astype(F32), 256, j * 128, iota)
    flow = dot_lanes(few_ref[...], cams_ref[...])
    back = flow[0:8, :]
    for n in range(1, PARTS):
        back = back + flow[8 * n : 8 * n + 8, :]
    return near_ref[...], back, scalar


OUT_SCRATCH = [
    pltpu.VMEM((128, 128), F32),
    pltpu.VMEM((PARTS, 128, 2048), BF16),
    pltpu.VMEM((128, 2048), BF16),
]
IN_SCRATCH = [
    pltpu.VMEM((32, 2048), BF16),
    pltpu.VMEM((256, 2048), BF16),
    pltpu.VMEM((8, 256), F32),
]


def block_product(system_ref, vector):
    return [
        sum(system_ref[LOOKUP[a, b] : LOOKUP[a, b] + 1, :] * vector[b] for b in range(6))
        for a in range(6)
    ]


def camera_kernel(
    recv_ref, index_ref, slots_ref, edge_ref, weight_ref, out_ref, system_ref, vector_ref,
    entry_ref, left_ref, hot_ref, sum_ref, turn_ref, edge_left_ref, edge_hot_ref,
):
    iota = iota_bf16(256)
    sum_ref[...] = jnp.zeros_like(sum_ref)
    entry_ref[27 * 8 : 32 * 8, :] = jnp.zeros((40, 128), F32)

    def build(t, side):
        base = pl.multiple_of(t * 8, 8)
        u, v, w, s00, s01, s11, f0, f1 = [
            recv_ref[pl.ds(base * 8 + r, 8, stride=8), :] for r in range(8)
        ]
        zero = jnp.zeros((8, 128), F32)
        uv = u * v
        top = [-uv, 1.0 + u * u, -v, w, zero, -u * w]
        low = [-1.0 - v * v, uv, u, zero, w, -v * w]
        g = [s00 * top[k] + s01 * low[k] for k in range(6)]
        h = [s01 * top[k] + s11 * low[k] for k in range(6)]
        for r, (a, b) in enumerate(SYMMETRIC_PAIRS):
            entry_ref[8 * r : 8 * r + 8, :] = top[a] * g[b] + low[a] * h[b]
        for a in range(6):
            entry_ref[8 * (21 + a) : 8 * (22 + a), :] = top[a] * f0 + low[a] * f1
        index = index_ref[pl.ds(base, 8), :].astype(F32)
        for i in range(8):
            onehot_rows(hot_ref.at[side], index[i : i + 1, :], 256, i * 128, iota)
            for n, part in enumerate(parts_of(entry_ref[pl.ds(i, 32, stride=8), :])):
                left_ref[side, n * 32 : (n + 1) * 32, i * 128 : (i + 1) * 128] = part.astype(BF16)

    def product(side):
        sum_ref[...] += dot_lanes(left_ref[side], hot_ref[side])

    build(0, 0)

    def pair(t, carry):
        build(2 * t + 1, 1)
        product(0)
        build(jnp.minimum(2 * t + 2, 15), 0)
        product(1)
        return carry

    lax.fori_loop(0, 8, pair, 0)
    summed = sum_ref[0:32, :]
    for n in range(1, PARTS):
        summed = summed + sum_ref[32 * n : 32 * n + 32, :]
    system_ref[0:32, :] = summed
    partial = jnp.zeros((1, 256), F32)
    for a in range(6):
        at = LOOKUP[a, a]
        diagonal = system_ref[at : at + 1, :] + DAMPING
        residual = -system_ref[21 + a : 22 + a, :]
        scaled = residual / diagonal
        partial = partial + residual * scaled
        vector_ref[a : a + 1, :] = scaled
    vector_ref[6:7, :] = jnp.ones((1, 256), F32)
    vector_ref[7:8, :] = jnp.broadcast_to(jnp.sum(partial, axis=1, keepdims=True), (1, 256))
    exchange_out(
        vector_ref, slots_ref, edge_ref, weight_ref, out_ref, turn_ref, edge_left_ref, edge_hot_ref
    )


def operator_rows(system_ref, vector_ref, degree, near, back):
    vector = [vector_ref[a : a + 1, :] for a in range(6)]
    own = block_product(system_ref, vector)
    return [
        own[a] + (DAMPING + degree) * vector[a] - near[a : a + 1, :] - back[a : a + 1, :]
        for a in range(6)
    ]


def first_kernel(
    recv_ref, system_ref, vector_ref, slots_ref, edge_ref, weight_ref, out_ref, image_ref, next_ref,
    turn_ref, left_ref, hot_ref, few_ref, cams_ref, near_ref,
):
    near, back, scalar = exchange_in(
        recv_ref, slots_ref, edge_ref, weight_ref, turn_ref, few_ref, cams_ref, near_ref
    )
    degree = jnp.sum(weight_ref[...], axis=0, keepdims=True) + back[6:7, :]
    image = operator_rows(system_ref, vector_ref, degree, near, back)
    partial = jnp.zeros((1, 256), F32)
    for a in range(6):
        at = LOOKUP[a, a]
        partial = partial + vector_ref[a : a + 1, :] * image[a]
        image_ref[a : a + 1, :] = image[a]
        next_ref[a : a + 1, :] = image[a] / (system_ref[at : at + 1, :] + DAMPING)
    image_ref[6:7, :] = degree
    image_ref[7:8, :] = jnp.broadcast_to(scalar, (1, 256))
    next_ref[6:7, :] = jnp.ones((1, 256), F32)
    next_ref[7:8, :] = jnp.broadcast_to(jnp.sum(partial, axis=1, keepdims=True), (1, 256))
    exchange_out(
        next_ref, slots_ref, edge_ref, weight_ref, out_ref, turn_ref, left_ref, hot_ref
    )


def second_kernel(
    recv_ref, system_ref, vector_ref, image_ref, next_ref, slots_ref, edge_ref, weight_ref,
    out_ref, state_ref, turn_ref, few_ref, cams_ref, near_ref,
):
    near, back, curvature = exchange_in(
        recv_ref, slots_ref, edge_ref, weight_ref, turn_ref, few_ref, cams_ref, near_ref
    )
    degree = image_ref[6:7, :]
    alpha = image_ref[7:8, :] / curvature
    image_next = operator_rows(system_ref, next_ref, degree, near, back)
    sums = [jnp.zeros((1, 256), F32) for _ in range(3)]
    for a in range(6):
        at = LOOKUP[a, a]
        vector, image = vector_ref[a : a + 1, :], image_ref[a : a + 1, :]
        residual = -system_ref[21 + a : 22 + a, :] - alpha * image
        scaled = residual / (system_ref[at : at + 1, :] + DAMPING)
        scaled_image = image - alpha * image_next[a]
        sums[0] = sums[0] + residual * scaled
        sums[1] = sums[1] + scaled * scaled_image
        sums[2] = sums[2] + scaled * image + vector * scaled_image
        state_ref[a : a + 1, :] = residual
        state_ref[8 + a : 9 + a, :] = scaled
        state_ref[16 + a : 17 + a, :] = scaled_image
    state_ref[6:7, :] = alpha
    state_ref[7:8, :] = jnp.broadcast_to(curvature, (1, 256))
    lane = lax.broadcasted_iota(jnp.int32, (128, 128), 1)
    rows = [jnp.sum(value, axis=1, keepdims=True) for value in sums]
    out_ref[...] = jnp.where(lane == 0, rows[0], jnp.where(lane == 1, rows[1], rows[2]))


def last_kernel(recv_ref, vector_ref, image_ref, state_ref, step_ref, residual_ref):
    sums = jnp.sum(recv_ref[...], axis=0, keepdims=True)
    fresh, inner, cross = sums[:, 0:1], sums[:, 1:2], sums[:, 2:3]
    alpha, curvature = state_ref[6:7, 0:1], state_ref[7:8, 0:1]
    beta = fresh / image_ref[7:8, 0:1]
    alpha_next = fresh / (inner + beta * cross + beta * beta * curvature)
    vector, image = vector_ref[0:6, :], image_ref[0:6, :]
    direction = state_ref[8:14, :] + beta * vector
    step_ref[...] = alpha * vector + alpha_next * direction
    residual_ref[...] = state_ref[0:6, :] - alpha_next * (state_ref[16:22, :] + beta * image)


def swap(payload):
    return lax.all_to_all(payload, AXES, split_axis=0, concat_axis=0, tiled=True)


def per_device(
    cam_pose, points, obs_uv, obs_cam, obs_pt, block_count, send_list, edge_slot, edge_weight
):
    cam_index = obs_cam.reshape(128, 128)
    point_index = obs_pt.reshape(128, 128)
    slots = jnp.transpose(send_list.reshape(128, 16))
    poses = call(pose_kernel, "poses", array(1024, 128), [pltpu.VMEM((8, 256), F32)])(
        cam_pose, cam_index, obs_uv.reshape(2, 128, 128)
    )
    arrived = swap(poses.reshape(128, 8, 128)).reshape(1024, 128)
    position = call(position_kernel, "positions", array(3, 128, 128))(points, point_index)
    reduced = call(
        eliminate_kernel,
        "eliminate",
        array(1024, 128),
        [
            pltpu.VMEM((9, 128, 128), F32),
            pltpu.VMEM((12, 128, 128), F32),
            pltpu.VMEM((2, 144 * PARTS, 1024), BF16),
            pltpu.VMEM((2, 256, 1024), BF16),
            pltpu.VMEM((144 * PARTS, 256), F32),
            pltpu.VMEM((144, 256), F32),
        ],
    )(arrived, position, point_index, block_count)
    returned = swap(reduced.reshape(128, 8, 128)).reshape(1024, 128)
    payload, system, vector = call(
        camera_kernel,
        "cameras",
        (array(128, 256), array(32, 256), array(8, 256)),
        [
            pltpu.VMEM((256, 128), F32),
            pltpu.VMEM((2, 32 * PARTS, 1024), BF16),
            pltpu.VMEM((2, 256, 1024), BF16),
            pltpu.VMEM((32 * PARTS, 256), F32),
        ]
        + OUT_SCRATCH,
    )(returned, cam_index, slots, edge_slot, edge_weight)
    payload, image, following = call(
        first_kernel,
        "first_product",
        (array(128, 256), array(8, 256), array(8, 256)),
        OUT_SCRATCH + IN_SCRATCH,
    )(swap(payload), system, vector, slots, edge_slot, edge_weight)
    payload, state = call(
        second_kernel,
        "second_product",
        (array(128, 128), array(24, 256)),
        [OUT_SCRATCH[0]] + IN_SCRATCH,
    )(swap(payload), system, vector, image, following, slots, edge_slot, edge_weight)
    return call(last_kernel, "last", (array(6, 256), array(6, 256)))(
        swap(payload.reshape(128, 1, 128)).reshape(128, 128), vector, image, state
    )


def solution(mesh):
    in_specs = (
        P(None, AXES),
        P(None, AXES),
        P(None, AXES, None, None),
        P(AXES, None, None),
        P(AXES, None, None),
        P(AXES, None),
        P(AXES, None, None),
        P(None, AXES),
        P(None, AXES),
    )
    out_specs = (P(None, AXES), P(None, AXES))
    return jax.shard_map(
        per_device, mesh=mesh, in_specs=in_specs, out_specs=out_specs, check_vma=False
    )
```

```python
import functools

import jax
import jax.numpy as jnp
from jax import lax
from jax.experimental import pallas as pl
from jax.experimental.pallas import tpu as pltpu
from jax.sharding import PartitionSpec as P

AXES = ("gx", "gy")
DAMPING = 1.0
SYMMETRIC_PAIRS = [(a, b) for a in range(6) for b in range(a, 6)]
LOOKUP = {}
for _place, (_a, _b) in enumerate(SYMMETRIC_PAIRS):
    LOOKUP[_a, _b] = _place
    LOOKUP[_b, _a] = _place
POINT_PAIRS = [(0, 0), (0, 1), (0, 2), (1, 1), (1, 2), (2, 2)]
PARTS = 2

F32 = jnp.float32
BF16 = jnp.bfloat16


def call(
    kernel, name, out_shape, scratch=(), flops=1_000_000, bytes_accessed=1_000_000, **specs
):
    return pl.pallas_call(
        kernel,
        out_shape=out_shape,
        **specs,
        scratch_shapes=list(scratch),
        name=name,
        compiler_params=pltpu.CompilerParams(vmem_limit_bytes=48 * 1024 * 1024),
        cost_estimate=pl.CostEstimate(
            flops=flops, bytes_accessed=bytes_accessed, transcendentals=0
        ),
    )


def array(*shape):
    return jax.ShapeDtypeStruct(shape, F32)


def take(table, index):
    return jnp.take_along_axis(table, index, axis=1, mode="promise_in_bounds")


def spread(row, count):
    return jnp.broadcast_to(row, (count, row.shape[1]))


def parts_of(value):
    parts = []
    for _ in range(PARTS):
        part = value.astype(BF16).astype(F32)
        value = value - part
        parts.append(part)
    return parts


def dot_lanes(left, right):
    return lax.dot_general(left, right, (((1,), (1,)), ((), ())), preferred_element_type=F32)


def pose_kernel(
    pose_hbm, cam_hbm, uv_hbm, out_ref, pose_ref, cam_ref, uv_ref, pose_sem, cam_sem, uv_sem
):
    copies = [
        pltpu.make_async_copy(pose_hbm, pose_ref, pose_sem),
        pltpu.make_async_copy(cam_hbm, cam_ref, cam_sem),
        pltpu.make_async_copy(uv_hbm, uv_ref, uv_sem),
    ]
    for copy in copies:
        copy.start()
    for copy in copies:
        copy.wait()
    inverse = 1.0 / pose_ref[0:1, :]
    pose_ref[1:4, :] = pose_ref[1:4, :] * inverse

    def tile(t, carry):
        base = pl.multiple_of(t * 8, 8)
        index = cam_ref[pl.ds(base, 8), :]
        lane, upper = index & 127, index >= 128
        for r in range(6):
            row = pose_ref[1 + r : 2 + r, :]
            out_ref[pl.ds(base * 8 + r, 8, stride=8), :] = jnp.where(
                upper,
                take(spread(row[:, 128:256], 8), lane),
                take(spread(row[:, 0:128], 8), lane),
            )
        for r in range(2):
            out_ref[pl.ds(base * 8 + 6 + r, 8, stride=8), :] = uv_ref[r, pl.ds(base, 8), :]
        return carry

    lax.fori_loop(0, 16, tile, 0, unroll=4)


def position_kernel(points_ref, index_ref, out_ref):
    def group(g, carry):
        base = pl.multiple_of(g * 32, 32)
        index = [index_ref[pl.ds(base + 8 * k, 8), :] for k in range(4)]
        lane = [value & 127 for value in index]
        chunk = [value >> 7 for value in index]
        found = [[jnp.zeros((8, 128), F32) for _ in range(4)] for _ in range(3)]
        for k in range(4):
            for h in range(32):
                for r in range(3):
                    row = spread(points_ref[r : r + 1, h * 128 : (h + 1) * 128], 8)
                    found[r][k] = jnp.where(chunk[k] == h, take(row, lane[k]), found[r][k])
        for r in range(3):
            for k in range(4):
                out_ref[r, pl.ds(base + 8 * k, 8), :] = found[r][k]
        return carry

    lax.fori_loop(0, 4, group, 0)


def onehot_rows(rows_ref, row, count, where, iota):
    value = spread(row, 16).astype(BF16)
    one, zero = jnp.ones((), BF16), jnp.zeros((), BF16)
    for q in range(count // 16):
        rows_ref[q * 16 : (q + 1) * 16, where : where + 128] = jnp.where(
            iota[q * 16 : (q + 1) * 16] == value, one, zero
        )


def iota_bf16(count):
    return lax.broadcasted_iota(jnp.int32, (count, 128), 0).astype(F32).astype(BF16)


def eliminate_kernel(
    recv_ref, position_ref, index_ref, count_ref, out_ref, term_ref, keep_ref, left_ref, hot_ref,
    sum_ref, half_ref, table_ref, ninth_ref, parts_ref, picked_ref, found_ref,
):
    live_count = jnp.transpose(spread(count_ref[0:1, :], 128))
    keep_ref[11, :, :] = jnp.where(
        lax.broadcasted_iota(jnp.int32, (128, 128), 1) < live_count, 1.0, 0.0
    )

    def prepare(t, carry):
        base = pl.multiple_of(t * 8, 8)
        row = [recv_ref[pl.ds(base * 8 + r, 8, stride=8), :] for r in range(8)]
        x = [position_ref[r, pl.ds(base, 8), :] for r in range(3)]
        live = keep_ref[11, pl.ds(base, 8), :]
        q1, q2, q3 = row[0], row[1], row[2]
        s1, s2, s3 = q1 * q1, q2 * q2, q3 * q3
        scale = 1.0 / (1.0 + s1 + s2 + s3)
        q12, q13, q23 = q1 * q2, q1 * q3, q2 * q3
        rot = [
            (1.0 + s1 - s2 - s3) * scale,
            2.0 * (q12 - q3) * scale,
            2.0 * (q13 + q2) * scale,
            2.0 * (q12 + q3) * scale,
            (1.0 - s1 + s2 - s3) * scale,
            2.0 * (q23 - q1) * scale,
            2.0 * (q13 - q2) * scale,
            2.0 * (q23 + q1) * scale,
            (1.0 - s1 - s2 + s3) * scale,
        ]
        cam = [
            rot[3 * a] * x[0] + rot[3 * a + 1] * x[1] + rot[3 * a + 2] * x[2] + row[3 + a]
            for a in range(3)
        ]
        inverse = 1.0 / cam[2]
        u, v = cam[0] * inverse, cam[1] * inverse
        residue = [(u - row[6]) * live, (v - row[7]) * live]
        scaled = inverse * live
        jac = [
            [scaled * (rot[k] - u * rot[6 + k]) for k in range(3)],
            [scaled * (rot[3 + k] - v * rot[6 + k]) for k in range(3)],
        ]
        terms = [jac[0][k] * jac[0][l] + jac[1][k] * jac[1][l] for k, l in POINT_PAIRS]
        terms += [jac[0][k] * residue[0] + jac[1][k] * residue[1] for k in range(3)]
        for r in range(9):
            term_ref[t, 8 * r : 8 * r + 8, :] = terms[r]
        for r, value in enumerate(jac[0] + jac[1] + residue + [u, v, inverse]):
            keep_ref[r, pl.ds(base, 8), :] = value
        return carry

    lax.fori_loop(0, 16, prepare, 0)

    iota_chunk, iota_lane = iota_bf16(16), iota_bf16(256)
    zero = jnp.zeros((), BF16)

    def build(t, side, half):
        index = index_ref[pl.ds(pl.multiple_of(t * 8, 8), 8), :]
        lane, chunk = (index & 255).astype(F32), (index >> 8).astype(F32)
        for i in range(8):
            at = half * 1024 + i * 128
            onehot_rows(hot_ref.at[t], lane[i : i + 1, :], 256, i * 128, iota_lane)
            where = spread(chunk[i : i + 1, :], 16).astype(BF16)
            both = jnp.concatenate(parts_of(term_ref[t, pl.ds(i, 8, stride=8), :]), 0).astype(BF16)
            for h in range(16):
                left_ref[side, h * 16 : (h + 1) * 16, at : at + 128] = jnp.where(
                    where == h, both, zero
                )
            mask = iota_chunk == where
            for n, part in enumerate(parts_of(term_ref[t, 64 + i : 65 + i, :])):
                left_ref[side, 256 + 16 * n : 272 + 16 * n, at : at + 128] = jnp.where(
                    mask, spread(part, 16).astype(BF16), zero
                )

    def build_two(g, side):
        build(2 * g, side, 0)
        build(2 * g + 1, side, 1)

    def hot_two(g):
        return jnp.concatenate([hot_ref[2 * g], hot_ref[2 * g + 1]], 1)

    def product(g, side):
        sum_ref[...] += dot_lanes(left_ref[side], hot_two(g))

    sum_ref[...] = jnp.zeros_like(sum_ref)
    build_two(0, 0)

    def pair(p, carry):
        build_two(2 * p + 1, 1)
        product(2 * p, 0)
        build_two(2 * p + 2, 0)
        product(2 * p + 1, 1)
        return carry

    lax.fori_loop(0, 3, pair, 0)
    build_two(7, 1)
    product(6, 0)
    product(7, 1)

    for side in range(2):
        lanes = slice(side * 128, side * 128 + 128)
        half_ref[...] = sum_ref[:, lanes]
        sums = [
            half_ref[pl.ds(r, 16, stride=16), :] + half_ref[pl.ds(8 + r, 16, stride=16), :]
            for r in range(8)
        ] + [half_ref[256:272, :] + half_ref[272:288, :]]
        hess = [sums[0] + DAMPING, sums[1], sums[2], sums[3] + DAMPING, sums[4], sums[5] + DAMPING]
        cofactor = [
            hess[3] * hess[5] - hess[4] * hess[4],
            hess[2] * hess[4] - hess[1] * hess[5],
            hess[1] * hess[4] - hess[2] * hess[3],
            hess[0] * hess[5] - hess[2] * hess[2],
            hess[1] * hess[2] - hess[0] * hess[4],
            hess[0] * hess[3] - hess[1] * hess[1],
        ]
        determinant = hess[0] * cofactor[0] + hess[1] * cofactor[1] + hess[2] * cofactor[2]
        inv = [value / determinant for value in cofactor]
        grad = sums[6:9]
        solved = [
            inv[0] * grad[0] + inv[1] * grad[1] + inv[2] * grad[2],
            inv[1] * grad[0] + inv[3] * grad[1] + inv[4] * grad[2],
            inv[2] * grad[0] + inv[4] * grad[1] + inv[5] * grad[2],
        ]
        for r, value in enumerate(inv + solved[0:2]):
            table_ref[pl.ds(r, 16, stride=8), :] = value
        ninth_ref[:, lanes] = solved[2]
        for h in range(16):
            parts_ref[h * 16 : (h + 1) * 16, lanes] = jnp.concatenate(
                parts_of(table_ref[8 * h : 8 * h + 8, :]), 0
            ).astype(BF16)

    def pick(g, side):
        picked_ref[side] = jnp.dot(parts_ref[...], hot_two(g), preferred_element_type=F32)

    def finish(t, side, half):
        base = pl.multiple_of(t * 8, 8)
        index = index_ref[pl.ds(base, 8), :]
        chunk = index >> 8
        for i in range(8):
            at = half * 1024 + i * 128
            where = spread(chunk[i : i + 1, :], 8)
            first, second = jnp.zeros((8, 128), F32), jnp.zeros((8, 128), F32)
            for h in range(16):
                first = jnp.where(
                    where == h, picked_ref[side, 16 * h : 16 * h + 8, at : at + 128], first
                )
                second = jnp.where(
                    where == h, picked_ref[side, 16 * h + 8 : 16 * h + 16, at : at + 128], second
                )
            found_ref[half, 8 * i : 8 * i + 8, :] = first + second
        lane, chunk = index & 127, index >> 7
        g2 = jnp.zeros((8, 128), F32)
        for h in range(32):
            row = ninth_ref[h // 2 : h // 2 + 1, (h % 2) * 128 : (h % 2) * 128 + 128]
            g2 = jnp.where(chunk == h, take(spread(row, 8), lane), g2)
        i0, i1, i2, i3, i4, i5, g0, g1 = [
            found_ref[half, pl.ds(r, 8, stride=8), :] for r in range(8)
        ]
        kept = [keep_ref[r, pl.ds(base, 8), :] for r in range(12)]
        p, q = kept[0:3], kept[3:6]
        pv = [
            i0 * p[0] + i1 * p[1] + i2 * p[2],
            i1 * p[0] + i3 * p[1] + i4 * p[2],
            i2 * p[0] + i4 * p[1] + i5 * p[2],
        ]
        qv = [
            i0 * q[0] + i1 * q[1] + i2 * q[2],
            i1 * q[0] + i3 * q[1] + i4 * q[2],
            i2 * q[0] + i4 * q[1] + i5 * q[2],
        ]
        live = kept[11]
        values = [
            kept[8],
            kept[9],
            kept[10],
            live - (pv[0] * p[0] + pv[1] * p[1] + pv[2] * p[2]),
            -(pv[0] * q[0] + pv[1] * q[1] + pv[2] * q[2]),
            live - (qv[0] * q[0] + qv[1] * q[1] + qv[2] * q[2]),
            kept[6] - (p[0] * g0 + p[1] * g1 + p[2] * g2),
            kept[7] - (q[0] * g0 + q[1] * g1 + q[2] * g2),
        ]
        for r, value in enumerate(values):
            out_ref[pl.ds(base * 8 + r, 8, stride=8), :] = value

    def finish_two(g, side):
        finish(2 * g, side, 0)
        finish(2 * g + 1, side, 1)

    pick(0, 0)

    def pick_pair(p, carry):
        pick(2 * p + 1, 1)
        finish_two(2 * p, 0)
        pick(2 * p + 2, 0)
        finish_two(2 * p + 1, 1)
        return carry

    lax.fori_loop(0, 3, pick_pair, 0)
    pick(7, 1)
    finish_two(6, 0)
    finish_two(7, 1)


def exchange_out(vector_ref, slots_ref, edge_ref, weight_ref, out_ref, turn_ref, left_ref, hot_ref):
    low, high = vector_ref[:, 0:128], vector_ref[:, 128:256]
    for j in range(16):
        index = spread(slots_ref[j : j + 1, :], 8)
        lane = index & 127
        turn_ref[8 * j : 8 * j + 8, :] = jnp.where(index >= 128, take(high, lane), take(low, lane))
    out_ref[pl.ds(0, 128, stride=2), :] = jnp.transpose(turn_ref[...])
    iota = iota_bf16(128)
    for k in range(8):
        for h in range(2):
            where = (2 * k + h) * 128
            edge = edge_ref[k : k + 1, h * 128 : (h + 1) * 128]
            onehot_rows(hot_ref, (edge >> 4).astype(F32), 128, where, iota)
            slot = spread(edge & 15, 8)
            weight = spread(weight_ref[k : k + 1, h * 128 : (h + 1) * 128], 8)
            for n, part in enumerate(parts_of(weight * (low, high)[h])):
                for j in range(0, 16, 2):
                    both = jnp.concatenate(
                        [jnp.where(slot == j, part, 0.0), jnp.where(slot == j + 1, part, 0.0)], 0
                    )
                    left_ref[n, 8 * j : 8 * j + 16, where : where + 128] = both.astype(BF16)
    summed = dot_lanes(hot_ref[...], left_ref[0])
    for n in range(1, PARTS):
        summed = summed + dot_lanes(hot_ref[...], left_ref[n])
    out_ref[pl.ds(1, 128, stride=2), :] = summed


def exchange_in(recv_ref, slots_ref, edge_ref, weight_ref, turn_ref, few_ref, cams_ref, near_ref):
    turn_ref[...] = jnp.transpose(recv_ref[pl.ds(0, 128, stride=2), :])
    for h in range(2):
        sums = jnp.zeros((8, 128), F32)
        for k in range(8):
            edge = edge_ref[k : k + 1, h * 128 : (h + 1) * 128]
            slot, peer = spread(edge & 15, 8), spread(edge >> 4, 8)
            near = jnp.zeros((8, 128), F32)
            for j in range(16):
                near = jnp.where(slot == j, take(turn_ref[8 * j : 8 * j + 8, :], peer), near)
            sums = sums + spread(weight_ref[k : k + 1, h * 128 : (h + 1) * 128], 8) * near
        near_ref[:, h * 128 : (h + 1) * 128] = sums
    scalar = jnp.sum(turn_ref[7:8, :], axis=1, keepdims=True)
    turn_ref[...] = jnp.transpose(recv_ref[pl.ds(1, 128, stride=2), :])
    iota = iota_bf16(256)
    for j in range(16):
        parts = parts_of(turn_ref[8 * j : 8 * j + 8, :])
        parts += [jnp.zeros((8, 128), F32)] * (4 - PARTS)
        few_ref[:, j * 128 : (j + 1) * 128] = jnp.concatenate(parts, 0).astype(BF16)
        onehot_rows(cams_ref, slots_ref[j : j + 1, :].astype(F32), 256, j * 128, iota)
    flow = dot_lanes(few_ref[...], cams_ref[...])
    back = flow[0:8, :]
    for n in range(1, PARTS):
        back = back + flow[8 * n : 8 * n + 8, :]
    return near_ref[...], back, scalar


OUT_SCRATCH = [
    pltpu.VMEM((128, 128), F32),
    pltpu.VMEM((PARTS, 128, 2048), BF16),
    pltpu.VMEM((128, 2048), BF16),
]
IN_SCRATCH = [
    pltpu.VMEM((32, 2048), BF16),
    pltpu.VMEM((256, 2048), BF16),
    pltpu.VMEM((8, 256), F32),
]


def block_product(system_ref, vector):
    return [
        sum(system_ref[LOOKUP[a, b] : LOOKUP[a, b] + 1, :] * vector[b] for b in range(6))
        for a in range(6)
    ]


def camera_kernel(
    recv_ref, index_ref, slots_ref, edge_ref, weight_ref, out_ref, system_ref, vector_ref,
    entry_ref, left_ref, hot_ref, sum_ref, turn_ref, edge_left_ref, edge_hot_ref,
):
    iota = iota_bf16(256)
    sum_ref[...] = jnp.zeros_like(sum_ref)
    entry_ref[:, 27 * 8 : 32 * 8, :] = jnp.zeros((2, 40, 128), F32)

    def build(t, side, half):
        base = pl.multiple_of(t * 8, 8)
        u, v, w, s00, s01, s11, f0, f1 = [
            recv_ref[pl.ds(base * 8 + r, 8, stride=8), :] for r in range(8)
        ]
        zero = jnp.zeros((8, 128), F32)
        uv = u * v
        top = [-uv, 1.0 + u * u, -v, w, zero, -u * w]
        low = [-1.0 - v * v, uv, u, zero, w, -v * w]
        g = [s00 * top[k] + s01 * low[k] for k in range(6)]
        h = [s01 * top[k] + s11 * low[k] for k in range(6)]
        for r, (a, b) in enumerate(SYMMETRIC_PAIRS):
            entry_ref[half, 8 * r : 8 * r + 8, :] = top[a] * g[b] + low[a] * h[b]
        for a in range(6):
            entry_ref[half, 8 * (21 + a) : 8 * (22 + a), :] = top[a] * f0 + low[a] * f1
        index = index_ref[pl.ds(base, 8), :].astype(F32)
        for i in range(8):
            onehot_rows(hot_ref.at[side], index[i : i + 1, :], 256, half * 1024 + i * 128, iota)
            at = half * 1024 + i * 128
            for n, part in enumerate(parts_of(entry_ref[half, pl.ds(i, 32, stride=8), :])):
                left_ref[side, n * 32 : (n + 1) * 32, at : at + 128] = part.astype(BF16)

    def build_two(g, side):
        build(2 * g, side, 0)
        build(2 * g + 1, side, 1)

    def product(side):
        sum_ref[...] += dot_lanes(left_ref[side], hot_ref[side])

    build_two(0, 0)

    def pair(p, carry):
        build_two(2 * p + 1, 1)
        product(0)
        build_two(2 * p + 2, 0)
        product(1)
        return carry

    lax.fori_loop(0, 3, pair, 0)
    build_two(7, 1)
    product(0)
    product(1)
    summed = sum_ref[0:32, :]
    for n in range(1, PARTS):
        summed = summed + sum_ref[32 * n : 32 * n + 32, :]
    system_ref[0:32, :] = summed
    partial = jnp.zeros((1, 256), F32)
    for a in range(6):
        at = LOOKUP[a, a]
        diagonal = system_ref[at : at + 1, :] + DAMPING
        residual = -system_ref[21 + a : 22 + a, :]
        scaled = residual / diagonal
        partial = partial + residual * scaled
        vector_ref[a : a + 1, :] = scaled
    vector_ref[6:7, :] = jnp.ones((1, 256), F32)
    vector_ref[7:8, :] = jnp.broadcast_to(jnp.sum(partial, axis=1, keepdims=True), (1, 256))
    exchange_out(
        vector_ref, slots_ref, edge_ref, weight_ref, out_ref, turn_ref, edge_left_ref, edge_hot_ref
    )


def operator_rows(system_ref, vector_ref, degree, near, back):
    vector = [vector_ref[a : a + 1, :] for a in range(6)]
    own = block_product(system_ref, vector)
    return [
        own[a] + (DAMPING + degree) * vector[a] - near[a : a + 1, :] - back[a : a + 1, :]
        for a in range(6)
    ]


def first_kernel(
    recv_ref, system_ref, vector_ref, slots_ref, edge_ref, weight_ref, out_ref, image_ref, next_ref,
    turn_ref, left_ref, hot_ref, few_ref, cams_ref, near_ref,
):
    near, back, scalar = exchange_in(
        recv_ref, slots_ref, edge_ref, weight_ref, turn_ref, few_ref, cams_ref, near_ref
    )
    degree = jnp.sum(weight_ref[...], axis=0, keepdims=True) + back[6:7, :]
    image = operator_rows(system_ref, vector_ref, degree, near, back)
    partial = jnp.zeros((1, 256), F32)
    for a in range(6):
        at = LOOKUP[a, a]
        partial = partial + vector_ref[a : a + 1, :] * image[a]
        image_ref[a : a + 1, :] = image[a]
        next_ref[a : a + 1, :] = image[a] / (system_ref[at : at + 1, :] + DAMPING)
    image_ref[6:7, :] = degree
    image_ref[7:8, :] = jnp.broadcast_to(scalar, (1, 256))
    next_ref[6:7, :] = jnp.ones((1, 256), F32)
    next_ref[7:8, :] = jnp.broadcast_to(jnp.sum(partial, axis=1, keepdims=True), (1, 256))
    exchange_out(
        next_ref, slots_ref, edge_ref, weight_ref, out_ref, turn_ref, left_ref, hot_ref
    )


def second_kernel(
    recv_ref, system_ref, vector_ref, image_ref, next_ref, slots_ref, edge_ref, weight_ref,
    out_ref, state_ref, turn_ref, few_ref, cams_ref, near_ref,
):
    near, back, curvature = exchange_in(
        recv_ref, slots_ref, edge_ref, weight_ref, turn_ref, few_ref, cams_ref, near_ref
    )
    degree = image_ref[6:7, :]
    alpha = image_ref[7:8, :] / curvature
    image_next = operator_rows(system_ref, next_ref, degree, near, back)
    sums = [jnp.zeros((1, 256), F32) for _ in range(3)]
    for a in range(6):
        at = LOOKUP[a, a]
        vector, image = vector_ref[a : a + 1, :], image_ref[a : a + 1, :]
        residual = -system_ref[21 + a : 22 + a, :] - alpha * image
        scaled = residual / (system_ref[at : at + 1, :] + DAMPING)
        scaled_image = image - alpha * image_next[a]
        sums[0] = sums[0] + residual * scaled
        sums[1] = sums[1] + scaled * scaled_image
        sums[2] = sums[2] + scaled * image + vector * scaled_image
        state_ref[a : a + 1, :] = residual
        state_ref[8 + a : 9 + a, :] = scaled
        state_ref[16 + a : 17 + a, :] = scaled_image
    state_ref[6:7, :] = alpha
    state_ref[7:8, :] = jnp.broadcast_to(curvature, (1, 256))
    lane = lax.broadcasted_iota(jnp.int32, (128, 128), 1)
    rows = [jnp.sum(value, axis=1, keepdims=True) for value in sums]
    out_ref[...] = jnp.where(lane == 0, rows[0], jnp.where(lane == 1, rows[1], rows[2]))


def last_kernel(recv_ref, vector_ref, image_ref, state_ref, step_ref, residual_ref):
    sums = jnp.sum(recv_ref[...], axis=0, keepdims=True)
    fresh, inner, cross = sums[:, 0:1], sums[:, 1:2], sums[:, 2:3]
    alpha, curvature = state_ref[6:7, 0:1], state_ref[7:8, 0:1]
    beta = fresh / image_ref[7:8, 0:1]
    alpha_next = fresh / (inner + beta * cross + beta * beta * curvature)
    vector, image = vector_ref[0:6, :], image_ref[0:6, :]
    direction = state_ref[8:14, :] + beta * vector
    step_ref[...] = alpha * vector + alpha_next * direction
    residual_ref[...] = state_ref[0:6, :] - alpha_next * (state_ref[16:22, :] + beta * image)


def kernels():
    vmem = pltpu.VMEM
    return {
        "poses": call(
            pose_kernel,
            "poses",
            array(1024, 128),
            [
                vmem((7, 256), F32),
                vmem((128, 128), jnp.int32),
                vmem((2, 128, 128), F32),
            ]
            + [pltpu.SemaphoreType.DMA] * 3,
            in_specs=[pl.BlockSpec(memory_space=pltpu.HBM)] * 3,
        ),
        "positions": call(position_kernel, "positions", array(3, 128, 128)),
        "eliminate": call(
            eliminate_kernel,
            "eliminate",
            array(1024, 128),
            [
                vmem((16, 72, 128), F32),
                vmem((12, 128, 128), F32),
                vmem((2, 288, 2048), BF16),
                vmem((16, 256, 1024), BF16),
                vmem((288, 256), F32),
                vmem((288, 128), F32),
                vmem((128, 128), F32),
                vmem((16, 256), F32),
                vmem((256, 256), BF16),
                vmem((2, 256, 2048), F32),
                vmem((2, 64, 128), F32),
            ],
        ),
        "cameras": call(
            camera_kernel,
            "cameras",
            (array(256, 128), array(32, 256), array(8, 256)),
            [
                vmem((2, 256, 128), F32),
                vmem((2, 32 * PARTS, 2048), BF16),
                vmem((2, 256, 2048), BF16),
                vmem((32 * PARTS, 256), F32),
            ]
            + OUT_SCRATCH,
        ),
        "first": call(
            first_kernel,
            "first_product",
            (array(256, 128), array(8, 256), array(8, 256)),
            OUT_SCRATCH + IN_SCRATCH,
        ),
        "second": call(
            second_kernel,
            "second_product",
            (array(128, 128), array(24, 256)),
            [OUT_SCRATCH[0]] + IN_SCRATCH,
        ),
        "last": call(last_kernel, "last", (array(6, 256), array(6, 256))),
    }


def swap(payload):
    blocks = payload.reshape(128, payload.shape[0] // 128, 128)
    return lax.all_to_all(blocks, AXES, split_axis=0, concat_axis=0, tiled=True).reshape(
        payload.shape
    )


def per_device(
    cam_pose, points, obs_uv, obs_cam, obs_pt, block_count, send_list, edge_slot, edge_weight
):
    run = kernels()
    cam_index = obs_cam.reshape(128, 128)
    point_index = obs_pt.reshape(128, 128)
    graph = (jnp.transpose(send_list.reshape(128, 16)), edge_slot, edge_weight)
    poses = run["poses"](cam_pose, cam_index, obs_uv.reshape(2, 128, 128))
    arrived = swap(poses)
    position = run["positions"](points, point_index)
    reduced = run["eliminate"](arrived, position, point_index, block_count)
    returned = swap(reduced)
    payload, system, vector = run["cameras"](returned, cam_index, *graph)
    payload, image, following = run["first"](swap(payload), system, vector, *graph)
    payload, state = run["second"](swap(payload), system, vector, image, following, *graph)
    return run["last"](swap(payload), vector, image, state)


def solution(mesh):
    in_specs = (
        P(None, AXES),
        P(None, AXES),
        P(None, AXES, None, None),
        P(AXES, None, None),
        P(AXES, None, None),
        P(AXES, None),
        P(AXES, None, None),
        P(None, AXES),
        P(None, AXES),
    )
    out_specs = (P(None, AXES), P(None, AXES))
    return jax.shard_map(
        per_device, mesh=mesh, in_specs=in_specs, out_specs=out_specs, check_vma=False
    )
```

```python
import functools

import jax
import jax.numpy as jnp
from jax import lax
from jax.experimental import pallas as pl
from jax.experimental.pallas import tpu as pltpu
from jax.sharding import PartitionSpec as P

AXES = ("gx", "gy")
DAMPING = 1.0
SYMMETRIC_PAIRS = [(a, b) for a in range(6) for b in range(a, 6)]
LOOKUP = {}
for _place, (_a, _b) in enumerate(SYMMETRIC_PAIRS):
    LOOKUP[_a, _b] = _place
    LOOKUP[_b, _a] = _place
POINT_PAIRS = [(0, 0), (0, 1), (0, 2), (1, 1), (1, 2), (2, 2)]
PARTS = 2

F32 = jnp.float32
BF16 = jnp.bfloat16


def call(
    kernel, name, out_shape, scratch=(), flops=1_000_000, bytes_accessed=1_000_000, vmem=48, **specs
):
    return pl.pallas_call(
        kernel,
        out_shape=out_shape,
        **specs,
        scratch_shapes=list(scratch),
        name=name,
        compiler_params=pltpu.CompilerParams(
            vmem_limit_bytes=vmem * 1024 * 1024 if vmem else None
        ),
        cost_estimate=pl.CostEstimate(
            flops=flops, bytes_accessed=bytes_accessed, transcendentals=0
        ),
    )


def array(*shape):
    return jax.ShapeDtypeStruct(shape, F32)


def take(table, index):
    return jnp.take_along_axis(table, index, axis=1, mode="promise_in_bounds")


def spread(row, count):
    return jnp.broadcast_to(row, (count, row.shape[1]))


def parts_of(value):
    parts = []
    for _ in range(PARTS):
        part = value.astype(BF16).astype(F32)
        value = value - part
        parts.append(part)
    return parts


def dot_lanes(left, right):
    return lax.dot_general(left, right, (((1,), (1,)), ((), ())), preferred_element_type=F32)


def pose_kernel(
    pose_hbm, cam_hbm, uv_hbm, out_ref, pose_ref, cam_ref, uv_ref, pose_sem, cam_sem, uv_sem
):
    copies = [
        pltpu.make_async_copy(pose_hbm, pose_ref, pose_sem),
        pltpu.make_async_copy(cam_hbm, cam_ref, cam_sem),
        pltpu.make_async_copy(uv_hbm, uv_ref, uv_sem),
    ]
    for copy in copies:
        copy.start()
    for copy in copies:
        copy.wait()
    inverse = 1.0 / pose_ref[0:1, :]
    pose_ref[1:4, :] = pose_ref[1:4, :] * inverse

    def tile(t, carry):
        base = pl.multiple_of(t * 8, 8)
        index = cam_ref[pl.ds(base, 8), :]
        lane, upper = index & 127, index >= 128
        for r in range(6):
            row = pose_ref[1 + r : 2 + r, :]
            out_ref[pl.ds(base * 8 + r, 8, stride=8), :] = jnp.where(
                upper,
                take(spread(row[:, 128:256], 8), lane),
                take(spread(row[:, 0:128], 8), lane),
            )
        for r in range(2):
            out_ref[pl.ds(base * 8 + 6 + r, 8, stride=8), :] = uv_ref[r, pl.ds(base, 8), :]
        return carry

    lax.fori_loop(0, 16, tile, 0, unroll=4)


def position_kernel(points_ref, index_ref, out_ref):
    def group(g, carry):
        base = pl.multiple_of(g * 32, 32)
        index = [index_ref[pl.ds(base + 8 * k, 8), :] for k in range(4)]
        lane = [value & 127 for value in index]
        chunk = [value >> 7 for value in index]
        found = [[jnp.zeros((8, 128), F32) for _ in range(4)] for _ in range(3)]
        for k in range(4):
            for h in range(32):
                for r in range(3):
                    row = spread(points_ref[r : r + 1, h * 128 : (h + 1) * 128], 8)
                    found[r][k] = jnp.where(chunk[k] == h, take(row, lane[k]), found[r][k])
        for r in range(3):
            for k in range(4):
                out_ref[r, pl.ds(base + 8 * k, 8), :] = found[r][k]
        return carry

    lax.fori_loop(0, 4, group, 0)


def onehot_rows(rows_ref, row, count, where, iota):
    value = spread(row, 16).astype(BF16)
    one, zero = jnp.ones((), BF16), jnp.zeros((), BF16)
    for q in range(count // 16):
        rows_ref[q * 16 : (q + 1) * 16, where : where + 128] = jnp.where(
            iota[q * 16 : (q + 1) * 16] == value, one, zero
        )


def iota_bf16(count):
    return lax.broadcasted_iota(jnp.int32, (count, 128), 0).astype(F32).astype(BF16)


def eliminate_kernel(
    recv_ref, position_ref, index_ref, count_ref, out_ref, term_ref, keep_ref, left_ref, hot_ref,
    sum_ref, half_ref, table_ref, ninth_ref, parts_ref, picked_ref, found_ref,
):
    live_count = jnp.transpose(spread(count_ref[0:1, :], 128))
    keep_ref[11, :, :] = jnp.where(
        lax.broadcasted_iota(jnp.int32, (128, 128), 1) < live_count, 1.0, 0.0
    )

    def prepare(t, carry):
        base = pl.multiple_of(t * 8, 8)
        row = [recv_ref[pl.ds(base * 8 + r, 8, stride=8), :] for r in range(8)]
        x = [position_ref[r, pl.ds(base, 8), :] for r in range(3)]
        live = keep_ref[11, pl.ds(base, 8), :]
        q1, q2, q3 = row[0], row[1], row[2]
        s1, s2, s3 = q1 * q1, q2 * q2, q3 * q3
        scale = 1.0 / (1.0 + s1 + s2 + s3)
        q12, q13, q23 = q1 * q2, q1 * q3, q2 * q3
        rot = [
            (1.0 + s1 - s2 - s3) * scale,
            2.0 * (q12 - q3) * scale,
            2.0 * (q13 + q2) * scale,
            2.0 * (q12 + q3) * scale,
            (1.0 - s1 + s2 - s3) * scale,
            2.0 * (q23 - q1) * scale,
            2.0 * (q13 - q2) * scale,
            2.0 * (q23 + q1) * scale,
            (1.0 - s1 - s2 + s3) * scale,
        ]
        cam = [
            rot[3 * a] * x[0] + rot[3 * a + 1] * x[1] + rot[3 * a + 2] * x[2] + row[3 + a]
            for a in range(3)
        ]
        inverse = 1.0 / cam[2]
        u, v = cam[0] * inverse, cam[1] * inverse
        residue = [(u - row[6]) * live, (v - row[7]) * live]
        scaled = inverse * live
        jac = [
            [scaled * (rot[k] - u * rot[6 + k]) for k in range(3)],
            [scaled * (rot[3 + k] - v * rot[6 + k]) for k in range(3)],
        ]
        terms = [jac[0][k] * jac[0][l] + jac[1][k] * jac[1][l] for k, l in POINT_PAIRS]
        terms += [jac[0][k] * residue[0] + jac[1][k] * residue[1] for k in range(3)]
        for r in range(9):
            term_ref[t, 8 * r : 8 * r + 8, :] = terms[r]
        for r, value in enumerate(jac[0] + jac[1] + residue + [u, v, inverse]):
            keep_ref[r, pl.ds(base, 8), :] = value
        return carry

    lax.fori_loop(0, 16, prepare, 0, unroll=4)

    iota_chunk, iota_lane = iota_bf16(16), iota_bf16(256)
    zero = jnp.zeros((), BF16)

    def build(t, side, half):
        index = index_ref[pl.ds(pl.multiple_of(t * 8, 8), 8), :]
        lane, chunk = (index & 255).astype(F32), (index >> 8).astype(F32)
        for i in range(8):
            at = half * 1024 + i * 128
            onehot_rows(hot_ref.at[t], lane[i : i + 1, :], 256, i * 128, iota_lane)
            where = spread(chunk[i : i + 1, :], 16).astype(BF16)
            both = jnp.concatenate(parts_of(term_ref[t, pl.ds(i, 8, stride=8), :]), 0).astype(BF16)
            for h in range(16):
                left_ref[side, h * 16 : (h + 1) * 16, at : at + 128] = jnp.where(
                    where == h, both, zero
                )
            mask = iota_chunk == where
            for n, part in enumerate(parts_of(term_ref[t, 64 + i : 65 + i, :])):
                left_ref[side, 256 + 16 * n : 272 + 16 * n, at : at + 128] = jnp.where(
                    mask, spread(part, 16).astype(BF16), zero
                )

    def build_two(g, side):
        build(2 * g, side, 0)
        build(2 * g + 1, side, 1)

    def hot_two(g):
        return jnp.concatenate([hot_ref[2 * g], hot_ref[2 * g + 1]], 1)

    def product(g, side):
        sum_ref[...] += dot_lanes(left_ref[side], hot_two(g))

    sum_ref[...] = jnp.zeros_like(sum_ref)
    build_two(0, 0)

    def pair(p, carry):
        build_two(2 * p + 1, 1)
        product(2 * p, 0)
        build_two(2 * p + 2, 0)
        product(2 * p + 1, 1)
        return carry

    lax.fori_loop(0, 3, pair, 0)
    build_two(7, 1)
    product(6, 0)
    product(7, 1)

    for side in range(2):
        lanes = slice(side * 128, side * 128 + 128)
        half_ref[...] = sum_ref[:, lanes]
        sums = [
            half_ref[pl.ds(r, 16, stride=16), :] + half_ref[pl.ds(8 + r, 16, stride=16), :]
            for r in range(8)
        ] + [half_ref[256:272, :] + half_ref[272:288, :]]
        hess = [sums[0] + DAMPING, sums[1], sums[2], sums[3] + DAMPING, sums[4], sums[5] + DAMPING]
        cofactor = [
            hess[3] * hess[5] - hess[4] * hess[4],
            hess[2] * hess[4] - hess[1] * hess[5],
            hess[1] * hess[4] - hess[2] * hess[3],
            hess[0] * hess[5] - hess[2] * hess[2],
            hess[1] * hess[2] - hess[0] * hess[4],
            hess[0] * hess[3] - hess[1] * hess[1],
        ]
        determinant = hess[0] * cofactor[0] + hess[1] * cofactor[1] + hess[2] * cofactor[2]
        inv = [value / determinant for value in cofactor]
        grad = sums[6:9]
        solved = [
            inv[0] * grad[0] + inv[1] * grad[1] + inv[2] * grad[2],
            inv[1] * grad[0] + inv[3] * grad[1] + inv[4] * grad[2],
            inv[2] * grad[0] + inv[4] * grad[1] + inv[5] * grad[2],
        ]
        for r, value in enumerate(inv + solved[0:2]):
            table_ref[pl.ds(r, 16, stride=8), :] = value
        ninth_ref[:, lanes] = solved[2]
        for h in range(16):
            parts_ref[h * 16 : (h + 1) * 16, lanes] = jnp.concatenate(
                parts_of(table_ref[8 * h : 8 * h + 8, :]), 0
            ).astype(BF16)

    def pick(g, side):
        picked_ref[side] = jnp.dot(parts_ref[...], hot_two(g), preferred_element_type=F32)

    def finish(t, side, half):
        base = pl.multiple_of(t * 8, 8)
        index = index_ref[pl.ds(base, 8), :]
        chunk = index >> 8
        for i in range(8):
            at = half * 1024 + i * 128
            where = spread(chunk[i : i + 1, :], 8)
            first, second = jnp.zeros((8, 128), F32), jnp.zeros((8, 128), F32)
            for h in range(16):
                first = jnp.where(
                    where == h, picked_ref[side, 16 * h : 16 * h + 8, at : at + 128], first
                )
                second = jnp.where(
                    where == h, picked_ref[side, 16 * h + 8 : 16 * h + 16, at : at + 128], second
                )
            found_ref[half, 8 * i : 8 * i + 8, :] = first + second
        lane, chunk = index & 127, index >> 7
        g2 = jnp.zeros((8, 128), F32)
        for h in range(32):
            row = ninth_ref[h // 2 : h // 2 + 1, (h % 2) * 128 : (h % 2) * 128 + 128]
            g2 = jnp.where(chunk == h, take(spread(row, 8), lane), g2)
        i0, i1, i2, i3, i4, i5, g0, g1 = [
            found_ref[half, pl.ds(r, 8, stride=8), :] for r in range(8)
        ]
        kept = [keep_ref[r, pl.ds(base, 8), :] for r in range(12)]
        p, q = kept[0:3], kept[3:6]
        pv = [
            i0 * p[0] + i1 * p[1] + i2 * p[2],
            i1 * p[0] + i3 * p[1] + i4 * p[2],
            i2 * p[0] + i4 * p[1] + i5 * p[2],
        ]
        qv = [
            i0 * q[0] + i1 * q[1] + i2 * q[2],
            i1 * q[0] + i3 * q[1] + i4 * q[2],
            i2 * q[0] + i4 * q[1] + i5 * q[2],
        ]
        live = kept[11]
        values = [
            kept[8],
            kept[9],
            kept[10],
            live - (pv[0] * p[0] + pv[1] * p[1] + pv[2] * p[2]),
            -(pv[0] * q[0] + pv[1] * q[1] + pv[2] * q[2]),
            live - (qv[0] * q[0] + qv[1] * q[1] + qv[2] * q[2]),
            kept[6] - (p[0] * g0 + p[1] * g1 + p[2] * g2),
            kept[7] - (q[0] * g0 + q[1] * g1 + q[2] * g2),
        ]
        for r, value in enumerate(values):
            out_ref[pl.ds(base * 8 + r, 8, stride=8), :] = value

    def finish_two(g, side):
        finish(2 * g, side, 0)
        finish(2 * g + 1, side, 1)

    pick(0, 0)

    def pick_pair(p, carry):
        pick(2 * p + 1, 1)
        finish_two(2 * p, 0)
        pick(2 * p + 2, 0)
        finish_two(2 * p + 1, 1)
        return carry

    lax.fori_loop(0, 3, pick_pair, 0)
    pick(7, 1)
    finish_two(6, 0)
    finish_two(7, 1)


def exchange_out(vector_ref, slots_ref, edge_ref, weight_ref, out_ref, turn_ref, left_ref, hot_ref):
    low, high = vector_ref[:, 0:128], vector_ref[:, 128:256]
    for j in range(16):
        index = spread(slots_ref[j : j + 1, :], 8)
        lane = index & 127
        turn_ref[8 * j : 8 * j + 8, :] = jnp.where(index >= 128, take(high, lane), take(low, lane))
    out_ref[pl.ds(0, 128, stride=2), :] = jnp.transpose(turn_ref[...])
    iota = iota_bf16(128)
    for k in range(8):
        for h in range(2):
            where = (2 * k + h) * 128
            edge = edge_ref[k : k + 1, h * 128 : (h + 1) * 128]
            onehot_rows(hot_ref, (edge >> 4).astype(F32), 128, where, iota)
            slot = spread(edge & 15, 8)
            weight = spread(weight_ref[k : k + 1, h * 128 : (h + 1) * 128], 8)
            for n, part in enumerate(parts_of(weight * (low, high)[h])):
                for j in range(0, 16, 2):
                    both = jnp.concatenate(
                        [jnp.where(slot == j, part, 0.0), jnp.where(slot == j + 1, part, 0.0)], 0
                    )
                    left_ref[n, 8 * j : 8 * j + 16, where : where + 128] = both.astype(BF16)
    summed = dot_lanes(hot_ref[...], left_ref[0])
    for n in range(1, PARTS):
        summed = summed + dot_lanes(hot_ref[...], left_ref[n])
    out_ref[pl.ds(1, 128, stride=2), :] = summed


def exchange_in(recv_ref, slots_ref, edge_ref, weight_ref, turn_ref, few_ref, cams_ref, near_ref):
    turn_ref[...] = jnp.transpose(recv_ref[pl.ds(0, 128, stride=2), :])
    for h in range(2):
        sums = jnp.zeros((8, 128), F32)
        for k in range(8):
            edge = edge_ref[k : k + 1, h * 128 : (h + 1) * 128]
            slot, peer = spread(edge & 15, 8), spread(edge >> 4, 8)
            near = jnp.zeros((8, 128), F32)
            for j in range(16):
                near = jnp.where(slot == j, take(turn_ref[8 * j : 8 * j + 8, :], peer), near)
            sums = sums + spread(weight_ref[k : k + 1, h * 128 : (h + 1) * 128], 8) * near
        near_ref[:, h * 128 : (h + 1) * 128] = sums
    scalar = jnp.sum(turn_ref[7:8, :], axis=1, keepdims=True)
    turn_ref[...] = jnp.transpose(recv_ref[pl.ds(1, 128, stride=2), :])
    iota = iota_bf16(256)
    for j in range(16):
        parts = parts_of(turn_ref[8 * j : 8 * j + 8, :])
        parts += [jnp.zeros((8, 128), F32)] * (4 - PARTS)
        few_ref[:, j * 128 : (j + 1) * 128] = jnp.concatenate(parts, 0).astype(BF16)
        onehot_rows(cams_ref, slots_ref[j : j + 1, :].astype(F32), 256, j * 128, iota)
    flow = dot_lanes(few_ref[...], cams_ref[...])
    back = flow[0:8, :]
    for n in range(1, PARTS):
        back = back + flow[8 * n : 8 * n + 8, :]
    return near_ref[...], back, scalar


OUT_SCRATCH = [
    pltpu.VMEM((128, 128), F32),
    pltpu.VMEM((PARTS, 128, 2048), BF16),
    pltpu.VMEM((128, 2048), BF16),
]
IN_SCRATCH = [
    pltpu.VMEM((32, 2048), BF16),
    pltpu.VMEM((256, 2048), BF16),
    pltpu.VMEM((8, 256), F32),
]


def block_product(system_ref, vector):
    return [
        sum(system_ref[LOOKUP[a, b] : LOOKUP[a, b] + 1, :] * vector[b] for b in range(6))
        for a in range(6)
    ]


def camera_kernel(
    recv_ref, index_ref, slots_ref, edge_ref, weight_ref, out_ref, system_ref, vector_ref,
    entry_ref, left_ref, hot_ref, sum_ref, turn_ref, edge_left_ref, edge_hot_ref,
):
    iota = iota_bf16(128)
    sum_ref[...] = jnp.zeros_like(sum_ref)
    entry_ref[:, 27 * 8 : 32 * 8, :] = jnp.zeros((2, 40, 128), F32)

    def build(t, side, half):
        base = pl.multiple_of(t * 8, 8)
        u, v, w, s00, s01, s11, f0, f1 = [
            recv_ref[pl.ds(base * 8 + r, 8, stride=8), :] for r in range(8)
        ]
        zero = jnp.zeros((8, 128), F32)
        uv = u * v
        top = [-uv, 1.0 + u * u, -v, w, zero, -u * w]
        low = [-1.0 - v * v, uv, u, zero, w, -v * w]
        g = [s00 * top[k] + s01 * low[k] for k in range(6)]
        h = [s01 * top[k] + s11 * low[k] for k in range(6)]
        for r, (a, b) in enumerate(SYMMETRIC_PAIRS):
            entry_ref[half, 8 * r : 8 * r + 8, :] = top[a] * g[b] + low[a] * h[b]
        for a in range(6):
            entry_ref[half, 8 * (21 + a) : 8 * (22 + a), :] = top[a] * f0 + low[a] * f1
        index = index_ref[pl.ds(base, 8), :]
        lane = (index & 127).astype(F32)
        for i in range(8):
            at = half * 1024 + i * 128
            onehot_rows(hot_ref.at[side], lane[i : i + 1, :], 128, at, iota)
            above = spread(index[i : i + 1, :], 32) >= 128
            for n, part in enumerate(parts_of(entry_ref[half, pl.ds(i, 32, stride=8), :])):
                left_ref[side, n * 32 : (n + 1) * 32, at : at + 128] = jnp.where(
                    above, 0.0, part
                ).astype(BF16)
                left_ref[side, 64 + n * 32 : 96 + n * 32, at : at + 128] = jnp.where(
                    above, part, 0.0
                ).astype(BF16)

    def build_two(g, side):
        build(2 * g, side, 0)
        build(2 * g + 1, side, 1)

    def product(side):
        sum_ref[...] += dot_lanes(left_ref[side], hot_ref[side])

    build_two(0, 0)

    def pair(p, carry):
        build_two(2 * p + 1, 1)
        product(0)
        build_two(2 * p + 2, 0)
        product(1)
        return carry

    lax.fori_loop(0, 3, pair, 0)
    build_two(7, 1)
    product(0)
    product(1)
    for h in range(2):
        at = 32 * PARTS * h
        system_ref[:, h * 128 : h * 128 + 128] = sum(
            sum_ref[at + 32 * n : at + 32 * n + 32, :] for n in range(PARTS)
        )
    partial = jnp.zeros((1, 256), F32)
    for a in range(6):
        at = LOOKUP[a, a]
        diagonal = system_ref[at : at + 1, :] + DAMPING
        residual = -system_ref[21 + a : 22 + a, :]
        scaled = residual / diagonal
        partial = partial + residual * scaled
        vector_ref[a : a + 1, :] = scaled
    vector_ref[6:7, :] = jnp.ones((1, 256), F32)
    vector_ref[7:8, :] = jnp.broadcast_to(jnp.sum(partial, axis=1, keepdims=True), (1, 256))
    exchange_out(
        vector_ref, slots_ref, edge_ref, weight_ref, out_ref, turn_ref, edge_left_ref, edge_hot_ref
    )


def operator_rows(system_ref, vector_ref, degree, near, back):
    vector = [vector_ref[a : a + 1, :] for a in range(6)]
    own = block_product(system_ref, vector)
    return [
        own[a] + (DAMPING + degree) * vector[a] - near[a : a + 1, :] - back[a : a + 1, :]
        for a in range(6)
    ]


def first_kernel(
    recv_ref, system_ref, vector_ref, slots_ref, edge_ref, weight_ref, out_ref, image_ref, next_ref,
    turn_ref, left_ref, hot_ref, few_ref, cams_ref, near_ref,
):
    near, back, scalar = exchange_in(
        recv_ref, slots_ref, edge_ref, weight_ref, turn_ref, few_ref, cams_ref, near_ref
    )
    degree = jnp.sum(weight_ref[...], axis=0, keepdims=True) + back[6:7, :]
    image = operator_rows(system_ref, vector_ref, degree, near, back)
    partial = jnp.zeros((1, 256), F32)
    for a in range(6):
        at = LOOKUP[a, a]
        partial = partial + vector_ref[a : a + 1, :] * image[a]
        image_ref[a : a + 1, :] = image[a]
        next_ref[a : a + 1, :] = image[a] / (system_ref[at : at + 1, :] + DAMPING)
    image_ref[6:7, :] = degree
    image_ref[7:8, :] = jnp.broadcast_to(scalar, (1, 256))
    next_ref[6:7, :] = jnp.ones((1, 256), F32)
    next_ref[7:8, :] = jnp.broadcast_to(jnp.sum(partial, axis=1, keepdims=True), (1, 256))
    exchange_out(
        next_ref, slots_ref, edge_ref, weight_ref, out_ref, turn_ref, left_ref, hot_ref
    )


def second_kernel(
    recv_ref, system_ref, vector_ref, image_ref, next_ref, slots_ref, edge_ref, weight_ref,
    out_ref, state_ref, turn_ref, few_ref, cams_ref, near_ref,
):
    near, back, curvature = exchange_in(
        recv_ref, slots_ref, edge_ref, weight_ref, turn_ref, few_ref, cams_ref, near_ref
    )
    degree = image_ref[6:7, :]
    alpha = image_ref[7:8, :] / curvature
    image_next = operator_rows(system_ref, next_ref, degree, near, back)
    sums = [jnp.zeros((1, 256), F32) for _ in range(3)]
    for a in range(6):
        at = LOOKUP[a, a]
        vector, image = vector_ref[a : a + 1, :], image_ref[a : a + 1, :]
        residual = -system_ref[21 + a : 22 + a, :] - alpha * image
        scaled = residual / (system_ref[at : at + 1, :] + DAMPING)
        scaled_image = image - alpha * image_next[a]
        sums[0] = sums[0] + residual * scaled
        sums[1] = sums[1] + scaled * scaled_image
        sums[2] = sums[2] + scaled * image + vector * scaled_image
        state_ref[a : a + 1, :] = residual
        state_ref[8 + a : 9 + a, :] = scaled
        state_ref[16 + a : 17 + a, :] = scaled_image
    state_ref[6:7, :] = alpha
    state_ref[7:8, :] = jnp.broadcast_to(curvature, (1, 256))
    lane = lax.broadcasted_iota(jnp.int32, (128, 128), 1)
    rows = [jnp.sum(value, axis=1, keepdims=True) for value in sums]
    out_ref[...] = jnp.where(lane == 0, rows[0], jnp.where(lane == 1, rows[1], rows[2]))


def last_kernel(recv_ref, vector_ref, image_ref, state_ref, step_ref, residual_ref):
    sums = jnp.sum(recv_ref[...], axis=0, keepdims=True)
    fresh, inner, cross = sums[:, 0:1], sums[:, 1:2], sums[:, 2:3]
    alpha, curvature = state_ref[6:7, 0:1], state_ref[7:8, 0:1]
    beta = fresh / image_ref[7:8, 0:1]
    alpha_next = fresh / (inner + beta * cross + beta * beta * curvature)
    vector, image = vector_ref[0:6, :], image_ref[0:6, :]
    direction = state_ref[8:14, :] + beta * vector
    step_ref[...] = alpha * vector + alpha_next * direction
    residual_ref[...] = state_ref[0:6, :] - alpha_next * (state_ref[16:22, :] + beta * image)


def kernels():
    vmem = pltpu.VMEM
    return {
        "poses": call(
            pose_kernel,
            "poses",
            array(1024, 128),
            [
                vmem((7, 256), F32),
                vmem((128, 128), jnp.int32),
                vmem((2, 128, 128), F32),
            ]
            + [pltpu.SemaphoreType.DMA] * 3,
            in_specs=[pl.BlockSpec(memory_space=pl.ANY)] * 3,
            vmem=None,
        ),
        "positions": call(position_kernel, "positions", array(3, 128, 128)),
        "eliminate": call(
            eliminate_kernel,
            "eliminate",
            array(1024, 128),
            [
                vmem((16, 72, 128), F32),
                vmem((12, 128, 128), F32),
                vmem((2, 288, 2048), BF16),
                vmem((16, 256, 1024), BF16),
                vmem((288, 256), F32),
                vmem((288, 128), F32),
                vmem((128, 128), F32),
                vmem((16, 256), F32),
                vmem((256, 256), BF16),
                vmem((2, 256, 2048), F32),
                vmem((2, 64, 128), F32),
            ],
        ),
        "cameras": call(
            camera_kernel,
            "cameras",
            (array(256, 128), array(32, 256), array(8, 256)),
            [
                vmem((2, 256, 128), F32),
                vmem((2, 64 * PARTS, 2048), BF16),
                vmem((2, 128, 2048), BF16),
                vmem((64 * PARTS, 128), F32),
            ]
            + OUT_SCRATCH,
        ),
        "first": call(
            first_kernel,
            "first_product",
            (array(256, 128), array(8, 256), array(8, 256)),
            OUT_SCRATCH + IN_SCRATCH,
        ),
        "second": call(
            second_kernel,
            "second_product",
            (array(128, 128), array(24, 256)),
            [OUT_SCRATCH[0]] + IN_SCRATCH,
        ),
        "last": call(last_kernel, "last", (array(6, 256), array(6, 256))),
    }


def swap(payload):
    blocks = payload.reshape(128, payload.shape[0] // 128, 128)
    return lax.all_to_all(blocks, AXES, split_axis=0, concat_axis=0, tiled=True).reshape(
        payload.shape
    )


def per_device(
    cam_pose, points, obs_uv, obs_cam, obs_pt, block_count, send_list, edge_slot, edge_weight
):
    run = kernels()
    cam_index = obs_cam.reshape(128, 128)
    point_index = obs_pt.reshape(128, 128)
    graph = (jnp.transpose(send_list.reshape(128, 16)), edge_slot, edge_weight)
    poses = run["poses"](cam_pose, cam_index, obs_uv.reshape(2, 128, 128))
    arrived = swap(poses)
    position = run["positions"](points, point_index)
    reduced = run["eliminate"](arrived, position, point_index, block_count)
    returned = swap(reduced)
    payload, system, vector = run["cameras"](returned, cam_index, *graph)
    payload, image, following = run["first"](swap(payload), system, vector, *graph)
    payload, state = run["second"](swap(payload), system, vector, image, following, *graph)
    return run["last"](swap(payload), vector, image, state)


def solution(mesh):
    in_specs = (
        P(None, AXES),
        P(None, AXES),
        P(None, AXES, None, None),
        P(AXES, None, None),
        P(AXES, None, None),
        P(AXES, None),
        P(AXES, None, None),
        P(None, AXES),
        P(None, AXES),
    )
    out_specs = (P(None, AXES), P(None, AXES))
    return jax.shard_map(
        per_device, mesh=mesh, in_specs=in_specs, out_specs=out_specs, check_vma=False
    )
```

```python
import functools

import jax
import jax.numpy as jnp
from jax import lax
from jax.experimental import pallas as pl
from jax.experimental.pallas import tpu as pltpu
from jax.sharding import PartitionSpec as P

AXES = ("gx", "gy")
DAMPING = 1.0
SYMMETRIC_PAIRS = [(a, b) for a in range(6) for b in range(a, 6)]
LOOKUP = {}
for _place, (_a, _b) in enumerate(SYMMETRIC_PAIRS):
    LOOKUP[_a, _b] = _place
    LOOKUP[_b, _a] = _place
POINT_PAIRS = [(0, 0), (0, 1), (0, 2), (1, 1), (1, 2), (2, 2)]
PARTS = 2

F32 = jnp.float32
BF16 = jnp.bfloat16


def call(
    kernel, name, out_shape, scratch=(), flops=1_000_000, bytes_accessed=1_000_000, vmem=48, **specs
):
    return pl.pallas_call(
        kernel,
        out_shape=out_shape,
        **specs,
        scratch_shapes=list(scratch),
        name=name,
        compiler_params=pltpu.CompilerParams(
            vmem_limit_bytes=vmem * 1024 * 1024 if vmem else None
        ),
        cost_estimate=pl.CostEstimate(
            flops=flops, bytes_accessed=bytes_accessed, transcendentals=0
        ),
    )


def array(*shape):
    return jax.ShapeDtypeStruct(shape, F32)


def eight(t):
    return t * 8 if isinstance(t, int) else pl.multiple_of(t * 8, 8)


def take(table, index):
    return jnp.take_along_axis(table, index, axis=1, mode="promise_in_bounds")


def spread(row, count):
    return jnp.broadcast_to(row, (count, row.shape[1]))


def parts_of(value):
    parts = []
    for _ in range(PARTS):
        part = value.astype(BF16).astype(F32)
        value = value - part
        parts.append(part)
    return parts


def dot_lanes(left, right):
    return lax.dot_general(left, right, (((1,), (1,)), ((), ())), preferred_element_type=F32)


def pose_kernel(
    pose_hbm, cam_hbm, uv_hbm, out_ref, pose_ref, cam_ref, uv_ref, pose_sem, cam_sem, uv_sem
):
    copies = [
        pltpu.make_async_copy(pose_hbm, pose_ref, pose_sem),
        pltpu.make_async_copy(cam_hbm, cam_ref, cam_sem),
        pltpu.make_async_copy(uv_hbm, uv_ref, uv_sem),
    ]
    for copy in copies:
        copy.start()
    for copy in copies:
        copy.wait()
    inverse = 1.0 / pose_ref[0:1, :]
    pose_ref[1:4, :] = pose_ref[1:4, :] * inverse

    def tile(t, carry):
        base = pl.multiple_of(t * 8, 8)
        index = cam_ref[pl.ds(base, 8), :]
        lane, upper = index & 127, index >= 128
        for r in range(6):
            row = pose_ref[1 + r : 2 + r, :]
            out_ref[pl.ds(base * 8 + r, 8, stride=8), :] = jnp.where(
                upper,
                take(spread(row[:, 128:256], 8), lane),
                take(spread(row[:, 0:128], 8), lane),
            )
        for r in range(2):
            out_ref[pl.ds(base * 8 + 6 + r, 8, stride=8), :] = uv_ref[r, pl.ds(base, 8), :]
        return carry

    lax.fori_loop(0, 16, tile, 0, unroll=4)


def position_kernel(points_ref, index_ref, out_ref):
    def group(g, carry):
        base = pl.multiple_of(g * 32, 32)
        index = [index_ref[pl.ds(base + 8 * k, 8), :] for k in range(4)]
        lane = [value & 127 for value in index]
        chunk = [value >> 7 for value in index]
        found = [[jnp.zeros((8, 128), F32) for _ in range(4)] for _ in range(3)]
        for k in range(4):
            for h in range(32):
                for r in range(3):
                    row = spread(points_ref[r : r + 1, h * 128 : (h + 1) * 128], 8)
                    found[r][k] = jnp.where(chunk[k] == h, take(row, lane[k]), found[r][k])
        for r in range(3):
            for k in range(4):
                out_ref[r, pl.ds(base + 8 * k, 8), :] = found[r][k]
        return carry

    lax.fori_loop(0, 4, group, 0)


def onehot_rows(rows_ref, row, count, where, iota):
    value = spread(row, 16).astype(BF16)
    one, zero = jnp.ones((), BF16), jnp.zeros((), BF16)
    for q in range(count // 16):
        rows_ref[q * 16 : (q + 1) * 16, where : where + 128] = jnp.where(
            iota[q * 16 : (q + 1) * 16] == value, one, zero
        )


def iota_bf16(count):
    return lax.broadcasted_iota(jnp.int32, (count, 128), 0).astype(F32).astype(BF16)


def eliminate_kernel(
    recv_ref, position_ref, index_ref, count_ref, out_ref, term_ref, keep_ref, left_ref, hot_ref,
    sum_ref, half_ref, table_ref, rest_ref, parts_ref, picked_ref, found_ref,
):
    live_count = jnp.transpose(spread(count_ref[0:1, :], 128))
    keep_ref[11, :, :] = jnp.where(
        lax.broadcasted_iota(jnp.int32, (128, 128), 1) < live_count, 1.0, 0.0
    )

    def prepare(t, carry):
        base = pl.multiple_of(t * 8, 8)
        row = [recv_ref[pl.ds(base * 8 + r, 8, stride=8), :] for r in range(8)]
        x = [position_ref[r, pl.ds(base, 8), :] for r in range(3)]
        live = keep_ref[11, pl.ds(base, 8), :]
        q1, q2, q3 = row[0], row[1], row[2]
        s1, s2, s3 = q1 * q1, q2 * q2, q3 * q3
        scale = 1.0 / (1.0 + s1 + s2 + s3)
        q12, q13, q23 = q1 * q2, q1 * q3, q2 * q3
        rot = [
            (1.0 + s1 - s2 - s3) * scale,
            2.0 * (q12 - q3) * scale,
            2.0 * (q13 + q2) * scale,
            2.0 * (q12 + q3) * scale,
            (1.0 - s1 + s2 - s3) * scale,
            2.0 * (q23 - q1) * scale,
            2.0 * (q13 - q2) * scale,
            2.0 * (q23 + q1) * scale,
            (1.0 - s1 - s2 + s3) * scale,
        ]
        cam = [
            rot[3 * a] * x[0] + rot[3 * a + 1] * x[1] + rot[3 * a + 2] * x[2] + row[3 + a]
            for a in range(3)
        ]
        inverse = 1.0 / cam[2]
        u, v = cam[0] * inverse, cam[1] * inverse
        residue = [(u - row[6]) * live, (v - row[7]) * live]
        scaled = inverse * live
        jac = [
            [scaled * (rot[k] - u * rot[6 + k]) for k in range(3)],
            [scaled * (rot[3 + k] - v * rot[6 + k]) for k in range(3)],
        ]
        terms = [jac[0][k] * jac[0][l] + jac[1][k] * jac[1][l] for k, l in POINT_PAIRS]
        terms += [jac[0][k] * residue[0] + jac[1][k] * residue[1] for k in range(3)]
        for r in range(9):
            term_ref[t, 8 * r : 8 * r + 8, :] = terms[r]
        for r, value in enumerate(jac[0] + jac[1] + residue + [u, v, inverse]):
            keep_ref[r, pl.ds(base, 8), :] = value
        return carry

    lax.fori_loop(0, 16, prepare, 0, unroll=4)

    iota_chunk, iota_lane = iota_bf16(16), iota_bf16(256)
    zero = jnp.zeros((), BF16)

    def build(t, side, half):
        index = index_ref[pl.ds(pl.multiple_of(t * 8, 8), 8), :]
        lane, chunk = (index & 255).astype(F32), (index >> 8).astype(F32)
        for i in range(8):
            at = half * 1024 + i * 128
            onehot_rows(hot_ref.at[t], lane[i : i + 1, :], 256, i * 128, iota_lane)
            where = spread(chunk[i : i + 1, :], 16).astype(BF16)
            both = jnp.concatenate(parts_of(term_ref[t, pl.ds(i, 8, stride=8), :]), 0).astype(BF16)
            for h in range(16):
                left_ref[side, h * 16 : (h + 1) * 16, at : at + 128] = jnp.where(
                    where == h, both, zero
                )
            mask = iota_chunk == where
            for n, part in enumerate(parts_of(term_ref[t, 64 + i : 65 + i, :])):
                left_ref[side, 256 + 16 * n : 272 + 16 * n, at : at + 128] = jnp.where(
                    mask, spread(part, 16).astype(BF16), zero
                )

    def build_two(g, side):
        build(2 * g, side, 0)
        build(2 * g + 1, side, 1)

    def hot_two(g):
        return jnp.concatenate([hot_ref[2 * g], hot_ref[2 * g + 1]], 1)

    def product(g, side):
        sum_ref[...] += dot_lanes(left_ref[side], hot_two(g))

    sum_ref[...] = jnp.zeros_like(sum_ref)
    build_two(0, 0)

    def pair(p, carry):
        build_two(2 * p + 1, 1)
        product(2 * p, 0)
        build_two(2 * p + 2, 0)
        product(2 * p + 1, 1)
        return carry

    lax.fori_loop(0, 3, pair, 0)
    build_two(7, 1)
    product(6, 0)
    product(7, 1)

    for side in range(2):
        lanes = slice(side * 128, side * 128 + 128)
        half_ref[...] = sum_ref[:, lanes]
        sums = [
            half_ref[pl.ds(r, 16, stride=16), :] + half_ref[pl.ds(8 + r, 16, stride=16), :]
            for r in range(8)
        ] + [half_ref[256:272, :] + half_ref[272:288, :]]
        hess = [sums[0] + DAMPING, sums[1], sums[2], sums[3] + DAMPING, sums[4], sums[5] + DAMPING]
        cofactor = [
            hess[3] * hess[5] - hess[4] * hess[4],
            hess[2] * hess[4] - hess[1] * hess[5],
            hess[1] * hess[4] - hess[2] * hess[3],
            hess[0] * hess[5] - hess[2] * hess[2],
            hess[1] * hess[2] - hess[0] * hess[4],
            hess[0] * hess[3] - hess[1] * hess[1],
        ]
        determinant = hess[0] * cofactor[0] + hess[1] * cofactor[1] + hess[2] * cofactor[2]
        inv = [value / determinant for value in cofactor]
        grad = sums[6:9]
        solved = [
            inv[0] * grad[0] + inv[1] * grad[1] + inv[2] * grad[2],
            inv[1] * grad[0] + inv[3] * grad[1] + inv[4] * grad[2],
            inv[2] * grad[0] + inv[4] * grad[1] + inv[5] * grad[2],
        ]
        for r, value in enumerate(inv[0:4]):
            table_ref[pl.ds(r, 16, stride=4), :] = value
        for r, value in enumerate(inv[4:6]):
            table_ref[pl.ds(64 + r, 16, stride=2), :] = value
        for r, value in enumerate(solved):
            rest_ref[16 * r : 16 * r + 16, lanes] = value
        for h in range(12):
            parts_ref[h * 16 : (h + 1) * 16, lanes] = jnp.concatenate(
                parts_of(table_ref[8 * h : 8 * h + 8, :]), 0
            ).astype(BF16)

    def pick(g, side):
        picked_ref[side] = jnp.dot(parts_ref[...], hot_two(g), preferred_element_type=F32)

    def finish(t, side, half):
        base = eight(t)
        index = index_ref[pl.ds(base, 8), :]
        chunk = index >> 8

        def rows_of(first_row, count, where, at):
            parts = [jnp.zeros((8, 128), F32) for _ in range(PARTS)]
            for h in range(count):
                for n in range(PARTS):
                    row = first_row + 16 * h + 8 * n
                    parts[n] = jnp.where(
                        where == h, picked_ref[side, row : row + 8, at : at + 128], parts[n]
                    )
            return parts[0] + parts[1]

        for i in range(8):
            at = half * 1024 + i * 128
            where = spread(chunk[i : i + 1, :], 8)
            four = rows_of(0, 8, where >> 1, at)
            odd = spread(chunk[i : i + 1, :], 4) & 1
            found_ref[half, 4 * i : 4 * i + 4, :] = jnp.where(
                odd == 1, four[4:8, :], four[0:4, :]
            )
            two = rows_of(128, 4, where >> 2, at)
            step = spread(chunk[i : i + 1, :], 2) & 3
            found_ref[half, 32 + 2 * i : 34 + 2 * i, :] = jnp.where(
                step >= 2,
                jnp.where(step == 3, two[6:8, :], two[4:6, :]),
                jnp.where(step == 1, two[2:4, :], two[0:2, :]),
            )
        lane, chunk = index & 127, index >> 7
        rest = [jnp.zeros((8, 128), F32) for _ in range(3)]
        for h in range(32):
            for r in range(3):
                at = 16 * r + h // 2
                row = rest_ref[at : at + 1, (h % 2) * 128 : (h % 2) * 128 + 128]
                rest[r] = jnp.where(chunk == h, take(spread(row, 8), lane), rest[r])
        g0, g1, g2 = rest
        i0, i1, i2, i3 = [found_ref[half, pl.ds(r, 8, stride=4), :] for r in range(4)]
        i4, i5 = [found_ref[half, pl.ds(32 + r, 8, stride=2), :] for r in range(2)]
        kept = [keep_ref[r, pl.ds(base, 8), :] for r in range(12)]
        p, q = kept[0:3], kept[3:6]
        pv = [
            i0 * p[0] + i1 * p[1] + i2 * p[2],
            i1 * p[0] + i3 * p[1] + i4 * p[2],
            i2 * p[0] + i4 * p[1] + i5 * p[2],
        ]
        qv = [
            i0 * q[0] + i1 * q[1] + i2 * q[2],
            i1 * q[0] + i3 * q[1] + i4 * q[2],
            i2 * q[0] + i4 * q[1] + i5 * q[2],
        ]
        live = kept[11]
        values = [
            kept[8],
            kept[9],
            kept[10],
            live - (pv[0] * p[0] + pv[1] * p[1] + pv[2] * p[2]),
            -(pv[0] * q[0] + pv[1] * q[1] + pv[2] * q[2]),
            live - (qv[0] * q[0] + qv[1] * q[1] + qv[2] * q[2]),
            kept[6] - (p[0] * g0 + p[1] * g1 + p[2] * g2),
            kept[7] - (q[0] * g0 + q[1] * g1 + q[2] * g2),
        ]
        for r, value in enumerate(values):
            out_ref[pl.ds(base * 8 + r, 8, stride=8), :] = value

    def finish_two(g, side):
        finish(2 * g, side, 0)
        finish(2 * g + 1, side, 1)

    pick(0, 0)

    def pick_pair(p, carry):
        pick(2 * p + 1, 1)
        finish_two(2 * p, 0)
        pick(2 * p + 2, 0)
        finish_two(2 * p + 1, 1)
        return carry

    for p in range(3):
        pick_pair(p, 0)
    pick(7, 1)
    finish_two(6, 0)
    finish_two(7, 1)


def exchange_out(vector_ref, slots_ref, edge_ref, weight_ref, out_ref, turn_ref, left_ref, hot_ref):
    low, high = vector_ref[:, 0:128], vector_ref[:, 128:256]
    for j in range(16):
        index = spread(slots_ref[j : j + 1, :], 8)
        lane = index & 127
        turn_ref[8 * j : 8 * j + 8, :] = jnp.where(index >= 128, take(high, lane), take(low, lane))
    out_ref[pl.ds(0, 128, stride=2), :] = jnp.transpose(turn_ref[...])
    iota = iota_bf16(128)
    for k in range(8):
        for h in range(2):
            where = (2 * k + h) * 128
            edge = edge_ref[k : k + 1, h * 128 : (h + 1) * 128]
            onehot_rows(hot_ref, (edge >> 4).astype(F32), 128, where, iota)
            slot = spread(edge & 15, 8)
            weight = spread(weight_ref[k : k + 1, h * 128 : (h + 1) * 128], 8)
            for n, part in enumerate(parts_of(weight * (low, high)[h])):
                for j in range(0, 16, 2):
                    both = jnp.concatenate(
                        [jnp.where(slot == j, part, 0.0), jnp.where(slot == j + 1, part, 0.0)], 0
                    )
                    left_ref[n, 8 * j : 8 * j + 16, where : where + 128] = both.astype(BF16)
    summed = dot_lanes(hot_ref[...], left_ref[0])
    for n in range(1, PARTS):
        summed = summed + dot_lanes(hot_ref[...], left_ref[n])
    out_ref[pl.ds(1, 128, stride=2), :] = summed


def exchange_in(recv_ref, slots_ref, edge_ref, weight_ref, turn_ref, few_ref, cams_ref, near_ref):
    turn_ref[...] = jnp.transpose(recv_ref[pl.ds(0, 128, stride=2), :])
    for h in range(2):
        sums = jnp.zeros((8, 128), F32)
        for k in range(8):
            edge = edge_ref[k : k + 1, h * 128 : (h + 1) * 128]
            slot, peer = spread(edge & 15, 8), spread(edge >> 4, 8)
            near = jnp.zeros((8, 128), F32)
            for j in range(16):
                near = jnp.where(slot == j, take(turn_ref[8 * j : 8 * j + 8, :], peer), near)
            sums = sums + spread(weight_ref[k : k + 1, h * 128 : (h + 1) * 128], 8) * near
        near_ref[:, h * 128 : (h + 1) * 128] = sums
    scalar = jnp.sum(turn_ref[7:8, :], axis=1, keepdims=True)
    turn_ref[...] = jnp.transpose(recv_ref[pl.ds(1, 128, stride=2), :])
    iota = iota_bf16(256)
    for j in range(16):
        parts = parts_of(turn_ref[8 * j : 8 * j + 8, :])
        parts += [jnp.zeros((8, 128), F32)] * (4 - PARTS)
        few_ref[:, j * 128 : (j + 1) * 128] = jnp.concatenate(parts, 0).astype(BF16)
        onehot_rows(cams_ref, slots_ref[j : j + 1, :].astype(F32), 256, j * 128, iota)
    flow = dot_lanes(few_ref[...], cams_ref[...])
    back = flow[0:8, :]
    for n in range(1, PARTS):
        back = back + flow[8 * n : 8 * n + 8, :]
    return near_ref[...], back, scalar


OUT_SCRATCH = [
    pltpu.VMEM((128, 128), F32),
    pltpu.VMEM((PARTS, 128, 2048), BF16),
    pltpu.VMEM((128, 2048), BF16),
]
IN_SCRATCH = [
    pltpu.VMEM((32, 2048), BF16),
    pltpu.VMEM((256, 2048), BF16),
    pltpu.VMEM((8, 256), F32),
]


def block_product(system_ref, vector):
    return [
        sum(system_ref[LOOKUP[a, b] : LOOKUP[a, b] + 1, :] * vector[b] for b in range(6))
        for a in range(6)
    ]


def camera_kernel(
    recv_ref, index_ref, slots_ref, edge_ref, weight_ref, out_ref, system_ref, vector_ref,
    entry_ref, left_ref, hot_ref, sum_ref, turn_ref, edge_left_ref, edge_hot_ref,
):
    iota = iota_bf16(128)
    sum_ref[...] = jnp.zeros_like(sum_ref)
    entry_ref[:, 27 * 8 : 32 * 8, :] = jnp.zeros((2, 40, 128), F32)

    def build(t, side, half):
        base = pl.multiple_of(t * 8, 8)
        u, v, w, s00, s01, s11, f0, f1 = [
            recv_ref[pl.ds(base * 8 + r, 8, stride=8), :] for r in range(8)
        ]
        zero = jnp.zeros((8, 128), F32)
        uv = u * v
        top = [-uv, 1.0 + u * u, -v, w, zero, -u * w]
        low = [-1.0 - v * v, uv, u, zero, w, -v * w]
        g = [s00 * top[k] + s01 * low[k] for k in range(6)]
        h = [s01 * top[k] + s11 * low[k] for k in range(6)]
        for r, (a, b) in enumerate(SYMMETRIC_PAIRS):
            entry_ref[half, 8 * r : 8 * r + 8, :] = top[a] * g[b] + low[a] * h[b]
        for a in range(6):
            entry_ref[half, 8 * (21 + a) : 8 * (22 + a), :] = top[a] * f0 + low[a] * f1
        index = index_ref[pl.ds(base, 8), :]
        lane = (index & 127).astype(F32)
        for i in range(8):
            at = half * 1024 + i * 128
            onehot_rows(hot_ref.at[side], lane[i : i + 1, :], 128, at, iota)
            above = spread(index[i : i + 1, :], 32) >= 128
            for n, part in enumerate(parts_of(entry_ref[half, pl.ds(i, 32, stride=8), :])):
                left_ref[side, n * 32 : (n + 1) * 32, at : at + 128] = jnp.where(
                    above, 0.0, part
                ).astype(BF16)
                left_ref[side, 64 + n * 32 : 96 + n * 32, at : at + 128] = jnp.where(
                    above, part, 0.0
                ).astype(BF16)

    def build_two(g, side):
        build(2 * g, side, 0)
        build(2 * g + 1, side, 1)

    def product(side):
        sum_ref[...] += dot_lanes(left_ref[side], hot_ref[side])

    build_two(0, 0)

    def pair(p, carry):
        build_two(2 * p + 1, 1)
        product(0)
        build_two(2 * p + 2, 0)
        product(1)
        return carry

    lax.fori_loop(0, 3, pair, 0)
    build_two(7, 1)
    product(0)
    product(1)
    for h in range(2):
        at = 32 * PARTS * h
        system_ref[:, h * 128 : h * 128 + 128] = sum(
            sum_ref[at + 32 * n : at + 32 * n + 32, :] for n in range(PARTS)
        )
    partial = jnp.zeros((1, 256), F32)
    for a in range(6):
        at = LOOKUP[a, a]
        diagonal = system_ref[at : at + 1, :] + DAMPING
        residual = -system_ref[21 + a : 22 + a, :]
        scaled = residual / diagonal
        partial = partial + residual * scaled
        vector_ref[a : a + 1, :] = scaled
    vector_ref[6:7, :] = jnp.ones((1, 256), F32)
    vector_ref[7:8, :] = jnp.broadcast_to(jnp.sum(partial, axis=1, keepdims=True), (1, 256))
    exchange_out(
        vector_ref, slots_ref, edge_ref, weight_ref, out_ref, turn_ref, edge_left_ref, edge_hot_ref
    )


def operator_rows(system_ref, vector_ref, degree, near, back):
    vector = [vector_ref[a : a + 1, :] for a in range(6)]
    own = block_product(system_ref, vector)
    return [
        own[a] + (DAMPING + degree) * vector[a] - near[a : a + 1, :] - back[a : a + 1, :]
        for a in range(6)
    ]


def first_kernel(
    recv_ref, system_ref, vector_ref, slots_ref, edge_ref, weight_ref, out_ref, image_ref, next_ref,
    turn_ref, left_ref, hot_ref, few_ref, cams_ref, near_ref,
):
    near, back, scalar = exchange_in(
        recv_ref, slots_ref, edge_ref, weight_ref, turn_ref, few_ref, cams_ref, near_ref
    )
    degree = jnp.sum(weight_ref[...], axis=0, keepdims=True) + back[6:7, :]
    image = operator_rows(system_ref, vector_ref, degree, near, back)
    partial = jnp.zeros((1, 256), F32)
    for a in range(6):
        at = LOOKUP[a, a]
        partial = partial + vector_ref[a : a + 1, :] * image[a]
        image_ref[a : a + 1, :] = image[a]
        next_ref[a : a + 1, :] = image[a] / (system_ref[at : at + 1, :] + DAMPING)
    image_ref[6:7, :] = degree
    image_ref[7:8, :] = jnp.broadcast_to(scalar, (1, 256))
    next_ref[6:7, :] = jnp.ones((1, 256), F32)
    next_ref[7:8, :] = jnp.broadcast_to(jnp.sum(partial, axis=1, keepdims=True), (1, 256))
    exchange_out(
        next_ref, slots_ref, edge_ref, weight_ref, out_ref, turn_ref, left_ref, hot_ref
    )


def second_kernel(
    recv_ref, system_ref, vector_ref, image_ref, next_ref, slots_ref, edge_ref, weight_ref,
    out_ref, state_ref, turn_ref, few_ref, cams_ref, near_ref,
):
    near, back, curvature = exchange_in(
        recv_ref, slots_ref, edge_ref, weight_ref, turn_ref, few_ref, cams_ref, near_ref
    )
    degree = image_ref[6:7, :]
    alpha = image_ref[7:8, :] / curvature
    image_next = operator_rows(system_ref, next_ref, degree, near, back)
    sums = [jnp.zeros((1, 256), F32) for _ in range(3)]
    for a in range(6):
        at = LOOKUP[a, a]
        vector, image = vector_ref[a : a + 1, :], image_ref[a : a + 1, :]
        residual = -system_ref[21 + a : 22 + a, :] - alpha * image
        scaled = residual / (system_ref[at : at + 1, :] + DAMPING)
        scaled_image = image - alpha * image_next[a]
        sums[0] = sums[0] + residual * scaled
        sums[1] = sums[1] + scaled * scaled_image
        sums[2] = sums[2] + scaled * image + vector * scaled_image
        state_ref[a : a + 1, :] = residual
        state_ref[8 + a : 9 + a, :] = scaled
        state_ref[16 + a : 17 + a, :] = scaled_image
    state_ref[6:7, :] = alpha
    state_ref[7:8, :] = jnp.broadcast_to(curvature, (1, 256))
    lane = lax.broadcasted_iota(jnp.int32, (128, 128), 1)
    rows = [jnp.sum(value, axis=1, keepdims=True) for value in sums]
    out_ref[...] = jnp.where(lane == 0, rows[0], jnp.where(lane == 1, rows[1], rows[2]))


def last_kernel(recv_ref, vector_ref, image_ref, state_ref, step_ref, residual_ref):
    sums = jnp.sum(recv_ref[...], axis=0, keepdims=True)
    fresh, inner, cross = sums[:, 0:1], sums[:, 1:2], sums[:, 2:3]
    alpha, curvature = state_ref[6:7, 0:1], state_ref[7:8, 0:1]
    beta = fresh / image_ref[7:8, 0:1]
    alpha_next = fresh / (inner + beta * cross + beta * beta * curvature)
    vector, image = vector_ref[0:6, :], image_ref[0:6, :]
    direction = state_ref[8:14, :] + beta * vector
    step_ref[...] = alpha * vector + alpha_next * direction
    residual_ref[...] = state_ref[0:6, :] - alpha_next * (state_ref[16:22, :] + beta * image)


def kernels():
    vmem = pltpu.VMEM
    return {
        "poses": call(
            pose_kernel,
            "poses",
            array(1024, 128),
            [
                vmem((7, 256), F32),
                vmem((128, 128), jnp.int32),
                vmem((2, 128, 128), F32),
            ]
            + [pltpu.SemaphoreType.DMA] * 3,
            in_specs=[pl.BlockSpec(memory_space=pl.ANY)] * 3,
            vmem=None,
        ),
        "positions": call(position_kernel, "positions", array(3, 128, 128)),
        "eliminate": call(
            eliminate_kernel,
            "eliminate",
            array(1024, 128),
            [
                vmem((16, 72, 128), F32),
                vmem((12, 128, 128), F32),
                vmem((2, 288, 2048), BF16),
                vmem((16, 256, 1024), BF16),
                vmem((288, 256), F32),
                vmem((288, 128), F32),
                vmem((96, 128), F32),
                vmem((48, 256), F32),
                vmem((192, 256), BF16),
                vmem((2, 192, 2048), F32),
                vmem((2, 48, 128), F32),
            ],
        ),
        "cameras": call(
            camera_kernel,
            "cameras",
            (array(256, 128), array(32, 256), array(8, 256)),
            [
                vmem((2, 256, 128), F32),
                vmem((2, 64 * PARTS, 2048), BF16),
                vmem((2, 128, 2048), BF16),
                vmem((64 * PARTS, 128), F32),
            ]
            + OUT_SCRATCH,
        ),
        "first": call(
            first_kernel,
            "first_product",
            (array(256, 128), array(8, 256), array(8, 256)),
            OUT_SCRATCH + IN_SCRATCH,
        ),
        "second": call(
            second_kernel,
            "second_product",
            (array(128, 128), array(24, 256)),
            [OUT_SCRATCH[0]] + IN_SCRATCH,
        ),
        "last": call(last_kernel, "last", (array(6, 256), array(6, 256))),
    }


def swap(payload):
    blocks = payload.reshape(128, payload.shape[0] // 128, 128)
    return lax.all_to_all(blocks, AXES, split_axis=0, concat_axis=0, tiled=True).reshape(
        payload.shape
    )


def per_device(
    cam_pose, points, obs_uv, obs_cam, obs_pt, block_count, send_list, edge_slot, edge_weight
):
    run = kernels()
    cam_index = obs_cam.reshape(128, 128)
    point_index = obs_pt.reshape(128, 128)
    graph = (jnp.transpose(send_list.reshape(128, 16)), edge_slot, edge_weight)
    poses = run["poses"](cam_pose, cam_index, obs_uv.reshape(2, 128, 128))
    arrived = swap(poses)
    position = run["positions"](points, point_index)
    reduced = run["eliminate"](arrived, position, point_index, block_count)
    returned = swap(reduced)
    payload, system, vector = run["cameras"](returned, cam_index, *graph)
    payload, image, following = run["first"](swap(payload), system, vector, *graph)
    payload, state = run["second"](swap(payload), system, vector, image, following, *graph)
    return run["last"](swap(payload), vector, image, state)


def solution(mesh):
    in_specs = (
        P(None, AXES),
        P(None, AXES),
        P(None, AXES, None, None),
        P(AXES, None, None),
        P(AXES, None, None),
        P(AXES, None),
        P(AXES, None, None),
        P(None, AXES),
        P(None, AXES),
    )
    out_specs = (P(None, AXES), P(None, AXES))
    return jax.shard_map(
        per_device, mesh=mesh, in_specs=in_specs, out_specs=out_specs, check_vma=False
    )
```

```python
import functools

import jax
import jax.numpy as jnp
from jax import lax
from jax.experimental import pallas as pl
from jax.experimental.pallas import tpu as pltpu
from jax.sharding import PartitionSpec as P

AXES = ("gx", "gy")
DAMPING = 1.0
SYMMETRIC_PAIRS = [(a, b) for a in range(6) for b in range(a, 6)]
LOOKUP = {}
for _place, (_a, _b) in enumerate(SYMMETRIC_PAIRS):
    LOOKUP[_a, _b] = _place
    LOOKUP[_b, _a] = _place
POINT_PAIRS = [(0, 0), (0, 1), (0, 2), (1, 1), (1, 2), (2, 2)]
PARTS = 2

F32 = jnp.float32
BF16 = jnp.bfloat16


def call(
    kernel, name, out_shape, scratch=(), flops=1_000_000, bytes_accessed=1_000_000, vmem=48, **specs
):
    return pl.pallas_call(
        kernel,
        out_shape=out_shape,
        **specs,
        scratch_shapes=list(scratch),
        name=name,
        compiler_params=pltpu.CompilerParams(
            vmem_limit_bytes=vmem * 1024 * 1024 if vmem else None
        ),
        cost_estimate=pl.CostEstimate(
            flops=flops, bytes_accessed=bytes_accessed, transcendentals=0
        ),
    )


def array(*shape):
    return jax.ShapeDtypeStruct(shape, F32)


def eight(t):
    return t * 8 if isinstance(t, int) else pl.multiple_of(t * 8, 8)


def take(table, index):
    return jnp.take_along_axis(table, index, axis=1, mode="promise_in_bounds")


def spread(row, count):
    return jnp.broadcast_to(row, (count, row.shape[1]))


def parts_of(value):
    parts = []
    for _ in range(PARTS):
        part = value.astype(BF16).astype(F32)
        value = value - part
        parts.append(part)
    return parts


def dot_lanes(left, right):
    return lax.dot_general(left, right, (((1,), (1,)), ((), ())), preferred_element_type=F32)


def pose_kernel(
    pose_hbm, cam_hbm, uv_hbm, out_ref, pose_ref, cam_ref, uv_ref, pose_sem, cam_sem, uv_sem
):
    copies = [
        pltpu.make_async_copy(pose_hbm, pose_ref, pose_sem),
        pltpu.make_async_copy(cam_hbm, cam_ref, cam_sem),
        pltpu.make_async_copy(uv_hbm, uv_ref, uv_sem),
    ]
    for copy in copies:
        copy.start()
    for copy in copies[0:2]:
        copy.wait()
    inverse = 1.0 / pose_ref[0:1, :]
    pose_ref[1:4, :] = pose_ref[1:4, :] * inverse

    def tile(t, carry):
        base = pl.multiple_of(t * 8, 8)
        index = cam_ref[pl.ds(base, 8), :]
        lane, upper = index & 127, index >= 128
        for r in range(6):
            row = pose_ref[1 + r : 2 + r, :]
            out_ref[pl.ds(base * 8 + r, 8, stride=8), :] = jnp.where(
                upper,
                take(spread(row[:, 128:256], 8), lane),
                take(spread(row[:, 0:128], 8), lane),
            )
        return carry

    lax.fori_loop(0, 16, tile, 0, unroll=8)
    copies[2].wait()

    def measured(t, carry):
        base = pl.multiple_of(t * 8, 8)
        for r in range(2):
            out_ref[pl.ds(base * 8 + 6 + r, 8, stride=8), :] = uv_ref[r, pl.ds(base, 8), :]
        return carry

    lax.fori_loop(0, 16, measured, 0, unroll=16)


def position_kernel(points_ref, index_ref, out_ref):
    def group(g, carry):
        base = pl.multiple_of(g * 32, 32)
        index = [index_ref[pl.ds(base + 8 * k, 8), :] for k in range(4)]
        lane = [value & 127 for value in index]
        chunk = [value >> 7 for value in index]
        found = [[jnp.zeros((8, 128), F32) for _ in range(4)] for _ in range(3)]
        for k in range(4):
            for h in range(32):
                for r in range(3):
                    row = spread(points_ref[r : r + 1, h * 128 : (h + 1) * 128], 8)
                    found[r][k] = jnp.where(chunk[k] == h, take(row, lane[k]), found[r][k])
        for r in range(3):
            for k in range(4):
                out_ref[r, pl.ds(base + 8 * k, 8), :] = found[r][k]
        return carry

    lax.fori_loop(0, 4, group, 0)


def onehot_rows(rows_ref, row, count, where, iota):
    value = spread(row, 16).astype(BF16)
    one, zero = jnp.ones((), BF16), jnp.zeros((), BF16)
    for q in range(count // 16):
        rows_ref[q * 16 : (q + 1) * 16, where : where + 128] = jnp.where(
            iota[q * 16 : (q + 1) * 16] == value, one, zero
        )


def iota_bf16(count):
    return lax.broadcasted_iota(jnp.int32, (count, 128), 0).astype(F32).astype(BF16)


def eliminate_kernel(
    recv_ref, position_ref, index_ref, count_ref, out_ref, term_ref, keep_ref, left_ref, hot_ref,
    sum_ref, half_ref, table_ref, rest_ref, parts_ref, picked_ref, found_ref,
):
    live_count = jnp.transpose(spread(count_ref[0:1, :], 128))
    keep_ref[11, :, :] = jnp.where(
        lax.broadcasted_iota(jnp.int32, (128, 128), 1) < live_count, 1.0, 0.0
    )

    def prepare(t, carry):
        base = pl.multiple_of(t * 8, 8)
        row = [recv_ref[pl.ds(base * 8 + r, 8, stride=8), :] for r in range(8)]
        x = [position_ref[r, pl.ds(base, 8), :] for r in range(3)]
        live = keep_ref[11, pl.ds(base, 8), :]
        q1, q2, q3 = row[0], row[1], row[2]
        s1, s2, s3 = q1 * q1, q2 * q2, q3 * q3
        scale = 1.0 / (1.0 + s1 + s2 + s3)
        q12, q13, q23 = q1 * q2, q1 * q3, q2 * q3
        rot = [
            (1.0 + s1 - s2 - s3) * scale,
            2.0 * (q12 - q3) * scale,
            2.0 * (q13 + q2) * scale,
            2.0 * (q12 + q3) * scale,
            (1.0 - s1 + s2 - s3) * scale,
            2.0 * (q23 - q1) * scale,
            2.0 * (q13 - q2) * scale,
            2.0 * (q23 + q1) * scale,
            (1.0 - s1 - s2 + s3) * scale,
        ]
        cam = [
            rot[3 * a] * x[0] + rot[3 * a + 1] * x[1] + rot[3 * a + 2] * x[2] + row[3 + a]
            for a in range(3)
        ]
        inverse = 1.0 / cam[2]
        u, v = cam[0] * inverse, cam[1] * inverse
        residue = [(u - row[6]) * live, (v - row[7]) * live]
        scaled = inverse * live
        jac = [
            [scaled * (rot[k] - u * rot[6 + k]) for k in range(3)],
            [scaled * (rot[3 + k] - v * rot[6 + k]) for k in range(3)],
        ]
        terms = [jac[0][k] * jac[0][l] + jac[1][k] * jac[1][l] for k, l in POINT_PAIRS]
        terms += [jac[0][k] * residue[0] + jac[1][k] * residue[1] for k in range(3)]
        for r in range(9):
            term_ref[t, 8 * r : 8 * r + 8, :] = terms[r]
        for r, value in enumerate(jac[0] + jac[1] + residue + [u, v, inverse]):
            keep_ref[r, pl.ds(base, 8), :] = value
        return carry

    lax.fori_loop(0, 16, prepare, 0, unroll=4)

    iota_chunk, iota_lane = iota_bf16(16), iota_bf16(256)
    zero = jnp.zeros((), BF16)

    def build(t, side, half):
        index = index_ref[pl.ds(pl.multiple_of(t * 8, 8), 8), :]
        lane, chunk = (index & 255).astype(F32), (index >> 8).astype(F32)
        for i in range(8):
            at = half * 1024 + i * 128
            onehot_rows(hot_ref.at[t], lane[i : i + 1, :], 256, i * 128, iota_lane)
            where = spread(chunk[i : i + 1, :], 16).astype(BF16)
            both = jnp.concatenate(parts_of(term_ref[t, pl.ds(i, 8, stride=8), :]), 0).astype(BF16)
            for h in range(16):
                left_ref[side, h * 16 : (h + 1) * 16, at : at + 128] = jnp.where(
                    where == h, both, zero
                )
            mask = iota_chunk == where
            for n, part in enumerate(parts_of(term_ref[t, 64 + i : 65 + i, :])):
                left_ref[side, 256 + 16 * n : 272 + 16 * n, at : at + 128] = jnp.where(
                    mask, spread(part, 16).astype(BF16), zero
                )

    def build_two(g, side):
        build(2 * g, side, 0)
        build(2 * g + 1, side, 1)

    def hot_two(g):
        return jnp.concatenate([hot_ref[2 * g], hot_ref[2 * g + 1]], 1)

    def product(g, side):
        sum_ref[...] += dot_lanes(left_ref[side], hot_two(g))

    sum_ref[...] = jnp.zeros_like(sum_ref)
    build_two(0, 0)

    def pair(p, carry):
        build_two(2 * p + 1, 1)
        product(2 * p, 0)
        build_two(2 * p + 2, 0)
        product(2 * p + 1, 1)
        return carry

    lax.fori_loop(0, 3, pair, 0)
    build_two(7, 1)
    product(6, 0)
    product(7, 1)

    for side in range(2):
        lanes = slice(side * 128, side * 128 + 128)
        half_ref[...] = sum_ref[:, lanes]
        sums = [
            half_ref[pl.ds(r, 16, stride=16), :] + half_ref[pl.ds(8 + r, 16, stride=16), :]
            for r in range(8)
        ] + [half_ref[256:272, :] + half_ref[272:288, :]]
        hess = [sums[0] + DAMPING, sums[1], sums[2], sums[3] + DAMPING, sums[4], sums[5] + DAMPING]
        cofactor = [
            hess[3] * hess[5] - hess[4] * hess[4],
            hess[2] * hess[4] - hess[1] * hess[5],
            hess[1] * hess[4] - hess[2] * hess[3],
            hess[0] * hess[5] - hess[2] * hess[2],
            hess[1] * hess[2] - hess[0] * hess[4],
            hess[0] * hess[3] - hess[1] * hess[1],
        ]
        determinant = hess[0] * cofactor[0] + hess[1] * cofactor[1] + hess[2] * cofactor[2]
        inv = [value / determinant for value in cofactor]
        grad = sums[6:9]
        solved = [
            inv[0] * grad[0] + inv[1] * grad[1] + inv[2] * grad[2],
            inv[1] * grad[0] + inv[3] * grad[1] + inv[4] * grad[2],
            inv[2] * grad[0] + inv[4] * grad[1] + inv[5] * grad[2],
        ]
        for r, value in enumerate(inv[0:4]):
            table_ref[pl.ds(r, 16, stride=4), :] = value
        for r, value in enumerate(inv[4:6]):
            table_ref[pl.ds(64 + r, 16, stride=2), :] = value
        for r, value in enumerate(solved):
            rest_ref[16 * r : 16 * r + 16, lanes] = value
        for h in range(12):
            parts_ref[h * 16 : (h + 1) * 16, lanes] = jnp.concatenate(
                parts_of(table_ref[8 * h : 8 * h + 8, :]), 0
            ).astype(BF16)

    def pick(g, side):
        picked_ref[side] = jnp.dot(parts_ref[...], hot_two(g), preferred_element_type=F32)

    def finish(t, side, half):
        base = eight(t)
        index = index_ref[pl.ds(base, 8), :]
        chunk = index >> 8

        def rows_of(first_row, count, where, at):
            parts = [jnp.zeros((8, 128), F32) for _ in range(PARTS)]
            for h in range(count):
                for n in range(PARTS):
                    row = first_row + 16 * h + 8 * n
                    parts[n] = jnp.where(
                        where == h, picked_ref[side, row : row + 8, at : at + 128], parts[n]
                    )
            return parts[0] + parts[1]

        for i in range(8):
            at = half * 1024 + i * 128
            where = spread(chunk[i : i + 1, :], 8)
            four = rows_of(0, 8, where >> 1, at)
            odd = spread(chunk[i : i + 1, :], 4) & 1
            found_ref[half, 4 * i : 4 * i + 4, :] = jnp.where(
                odd == 1, four[4:8, :], four[0:4, :]
            )
            two = rows_of(128, 4, where >> 2, at)
            step = spread(chunk[i : i + 1, :], 2) & 3
            found_ref[half, 32 + 2 * i : 34 + 2 * i, :] = jnp.where(
                step >= 2,
                jnp.where(step == 3, two[6:8, :], two[4:6, :]),
                jnp.where(step == 1, two[2:4, :], two[0:2, :]),
            )
        lane, chunk = index & 127, index >> 7
        rest = [jnp.zeros((8, 128), F32) for _ in range(3)]
        for h in range(32):
            for r in range(3):
                at = 16 * r + h // 2
                row = rest_ref[at : at + 1, (h % 2) * 128 : (h % 2) * 128 + 128]
                rest[r] = jnp.where(chunk == h, take(spread(row, 8), lane), rest[r])
        g0, g1, g2 = rest
        i0, i1, i2, i3 = [found_ref[half, pl.ds(r, 8, stride=4), :] for r in range(4)]
        i4, i5 = [found_ref[half, pl.ds(32 + r, 8, stride=2), :] for r in range(2)]
        kept = [keep_ref[r, pl.ds(base, 8), :] for r in range(12)]
        p, q = kept[0:3], kept[3:6]
        pv = [
            i0 * p[0] + i1 * p[1] + i2 * p[2],
            i1 * p[0] + i3 * p[1] + i4 * p[2],
            i2 * p[0] + i4 * p[1] + i5 * p[2],
        ]
        qv = [
            i0 * q[0] + i1 * q[1] + i2 * q[2],
            i1 * q[0] + i3 * q[1] + i4 * q[2],
            i2 * q[0] + i4 * q[1] + i5 * q[2],
        ]
        live = kept[11]
        values = [
            kept[8],
            kept[9],
            kept[10],
            live - (pv[0] * p[0] + pv[1] * p[1] + pv[2] * p[2]),
            -(pv[0] * q[0] + pv[1] * q[1] + pv[2] * q[2]),
            live - (qv[0] * q[0] + qv[1] * q[1] + qv[2] * q[2]),
            kept[6] - (p[0] * g0 + p[1] * g1 + p[2] * g2),
            kept[7] - (q[0] * g0 + q[1] * g1 + q[2] * g2),
        ]
        for r, value in enumerate(values):
            out_ref[pl.ds(base * 8 + r, 8, stride=8), :] = value

    def finish_two(g, side):
        finish(2 * g, side, 0)
        finish(2 * g + 1, side, 1)

    pick(0, 0)

    def pick_pair(p, carry):
        pick(2 * p + 1, 1)
        finish_two(2 * p, 0)
        pick(2 * p + 2, 0)
        finish_two(2 * p + 1, 1)
        return carry

    for p in range(3):
        pick_pair(p, 0)
    pick(7, 1)
    finish_two(6, 0)
    finish_two(7, 1)


def exchange_out(vector_ref, slots_ref, edge_ref, weight_ref, out_ref, turn_ref, left_ref, hot_ref):
    low, high = vector_ref[:, 0:128], vector_ref[:, 128:256]
    for j in range(16):
        index = spread(slots_ref[j : j + 1, :], 8)
        lane = index & 127
        turn_ref[8 * j : 8 * j + 8, :] = jnp.where(index >= 128, take(high, lane), take(low, lane))
    out_ref[pl.ds(0, 128, stride=2), :] = jnp.transpose(turn_ref[...])
    iota = iota_bf16(128)
    for k in range(8):
        for h in range(2):
            where = (2 * k + h) * 128
            edge = edge_ref[k : k + 1, h * 128 : (h + 1) * 128]
            onehot_rows(hot_ref, (edge >> 4).astype(F32), 128, where, iota)
            slot = spread(edge & 15, 8)
            weight = spread(weight_ref[k : k + 1, h * 128 : (h + 1) * 128], 8)
            for n, part in enumerate(parts_of(weight * (low, high)[h])):
                for j in range(0, 16, 2):
                    both = jnp.concatenate(
                        [jnp.where(slot == j, part, 0.0), jnp.where(slot == j + 1, part, 0.0)], 0
                    )
                    left_ref[n, 8 * j : 8 * j + 16, where : where + 128] = both.astype(BF16)
    summed = dot_lanes(hot_ref[...], left_ref[0])
    for n in range(1, PARTS):
        summed = summed + dot_lanes(hot_ref[...], left_ref[n])
    out_ref[pl.ds(1, 128, stride=2), :] = summed


def exchange_in(recv_ref, slots_ref, edge_ref, weight_ref, turn_ref, few_ref, cams_ref, near_ref):
    turn_ref[...] = jnp.transpose(recv_ref[pl.ds(0, 128, stride=2), :])
    for h in range(2):
        sums = jnp.zeros((8, 128), F32)
        for k in range(8):
            edge = edge_ref[k : k + 1, h * 128 : (h + 1) * 128]
            slot, peer = spread(edge & 15, 8), spread(edge >> 4, 8)
            near = jnp.zeros((8, 128), F32)
            for j in range(16):
                near = jnp.where(slot == j, take(turn_ref[8 * j : 8 * j + 8, :], peer), near)
            sums = sums + spread(weight_ref[k : k + 1, h * 128 : (h + 1) * 128], 8) * near
        near_ref[:, h * 128 : (h + 1) * 128] = sums
    scalar = jnp.sum(turn_ref[7:8, :], axis=1, keepdims=True)
    turn_ref[...] = jnp.transpose(recv_ref[pl.ds(1, 128, stride=2), :])
    iota = iota_bf16(256)
    for j in range(16):
        parts = parts_of(turn_ref[8 * j : 8 * j + 8, :])
        parts += [jnp.zeros((8, 128), F32)] * (4 - PARTS)
        few_ref[:, j * 128 : (j + 1) * 128] = jnp.concatenate(parts, 0).astype(BF16)
        onehot_rows(cams_ref, slots_ref[j : j + 1, :].astype(F32), 256, j * 128, iota)
    flow = dot_lanes(few_ref[...], cams_ref[...])
    back = flow[0:8, :]
    for n in range(1, PARTS):
        back = back + flow[8 * n : 8 * n + 8, :]
    return near_ref[...], back, scalar


OUT_SCRATCH = [
    pltpu.VMEM((128, 128), F32),
    pltpu.VMEM((PARTS, 128, 2048), BF16),
    pltpu.VMEM((128, 2048), BF16),
]
IN_SCRATCH = [
    pltpu.VMEM((32, 2048), BF16),
    pltpu.VMEM((256, 2048), BF16),
    pltpu.VMEM((8, 256), F32),
]


def block_product(system_ref, vector):
    return [
        sum(system_ref[LOOKUP[a, b] : LOOKUP[a, b] + 1, :] * vector[b] for b in range(6))
        for a in range(6)
    ]


def camera_kernel(
    recv_ref, index_ref, slots_ref, edge_ref, weight_ref, out_ref, system_ref, vector_ref,
    entry_ref, left_ref, hot_ref, sum_ref, turn_ref, edge_left_ref, edge_hot_ref,
):
    iota = iota_bf16(128)
    sum_ref[...] = jnp.zeros_like(sum_ref)
    entry_ref[:, 27 * 8 : 32 * 8, :] = jnp.zeros((2, 40, 128), F32)

    def build(t, side, half):
        base = pl.multiple_of(t * 8, 8)
        u, v, w, s00, s01, s11, f0, f1 = [
            recv_ref[pl.ds(base * 8 + r, 8, stride=8), :] for r in range(8)
        ]
        zero = jnp.zeros((8, 128), F32)
        uv = u * v
        top = [-uv, 1.0 + u * u, -v, w, zero, -u * w]
        low = [-1.0 - v * v, uv, u, zero, w, -v * w]
        g = [s00 * top[k] + s01 * low[k] for k in range(6)]
        h = [s01 * top[k] + s11 * low[k] for k in range(6)]
        for r, (a, b) in enumerate(SYMMETRIC_PAIRS):
            entry_ref[half, 8 * r : 8 * r + 8, :] = top[a] * g[b] + low[a] * h[b]
        for a in range(6):
            entry_ref[half, 8 * (21 + a) : 8 * (22 + a), :] = top[a] * f0 + low[a] * f1
        index = index_ref[pl.ds(base, 8), :]
        lane = (index & 127).astype(F32)
        for i in range(8):
            at = half * 1024 + i * 128
            onehot_rows(hot_ref.at[side], lane[i : i + 1, :], 128, at, iota)
            above = spread(index[i : i + 1, :], 32) >= 128
            for n, part in enumerate(parts_of(entry_ref[half, pl.ds(i, 32, stride=8), :])):
                left_ref[side, n * 32 : (n + 1) * 32, at : at + 128] = jnp.where(
                    above, 0.0, part
                ).astype(BF16)
                left_ref[side, 64 + n * 32 : 96 + n * 32, at : at + 128] = jnp.where(
                    above, part, 0.0
                ).astype(BF16)

    def build_two(g, side):
        build(2 * g, side, 0)
        build(2 * g + 1, side, 1)

    def product(side):
        sum_ref[...] += dot_lanes(left_ref[side], hot_ref[side])

    build_two(0, 0)

    def pair(p, carry):
        build_two(2 * p + 1, 1)
        product(0)
        build_two(2 * p + 2, 0)
        product(1)
        return carry

    lax.fori_loop(0, 3, pair, 0)
    build_two(7, 1)
    product(0)
    product(1)
    for h in range(2):
        at = 32 * PARTS * h
        system_ref[:, h * 128 : h * 128 + 128] = sum(
            sum_ref[at + 32 * n : at + 32 * n + 32, :] for n in range(PARTS)
        )
    partial = jnp.zeros((1, 256), F32)
    for a in range(6):
        at = LOOKUP[a, a]
        diagonal = system_ref[at : at + 1, :] + DAMPING
        residual = -system_ref[21 + a : 22 + a, :]
        scaled = residual / diagonal
        partial = partial + residual * scaled
        vector_ref[a : a + 1, :] = scaled
    vector_ref[6:7, :] = jnp.ones((1, 256), F32)
    vector_ref[7:8, :] = jnp.broadcast_to(jnp.sum(partial, axis=1, keepdims=True), (1, 256))
    exchange_out(
        vector_ref, slots_ref, edge_ref, weight_ref, out_ref, turn_ref, edge_left_ref, edge_hot_ref
    )


def operator_rows(system_ref, vector_ref, degree, near, back):
    vector = [vector_ref[a : a + 1, :] for a in range(6)]
    own = block_product(system_ref, vector)
    return [
        own[a] + (DAMPING + degree) * vector[a] - near[a : a + 1, :] - back[a : a + 1, :]
        for a in range(6)
    ]


def first_kernel(
    recv_ref, system_ref, vector_ref, slots_ref, edge_ref, weight_ref, out_ref, image_ref, next_ref,
    turn_ref, left_ref, hot_ref, few_ref, cams_ref, near_ref,
):
    near, back, scalar = exchange_in(
        recv_ref, slots_ref, edge_ref, weight_ref, turn_ref, few_ref, cams_ref, near_ref
    )
    degree = jnp.sum(weight_ref[...], axis=0, keepdims=True) + back[6:7, :]
    image = operator_rows(system_ref, vector_ref, degree, near, back)
    partial = jnp.zeros((1, 256), F32)
    for a in range(6):
        at = LOOKUP[a, a]
        partial = partial + vector_ref[a : a + 1, :] * image[a]
        image_ref[a : a + 1, :] = image[a]
        next_ref[a : a + 1, :] = image[a] / (system_ref[at : at + 1, :] + DAMPING)
    image_ref[6:7, :] = degree
    image_ref[7:8, :] = jnp.broadcast_to(scalar, (1, 256))
    next_ref[6:7, :] = jnp.ones((1, 256), F32)
    next_ref[7:8, :] = jnp.broadcast_to(jnp.sum(partial, axis=1, keepdims=True), (1, 256))
    exchange_out(
        next_ref, slots_ref, edge_ref, weight_ref, out_ref, turn_ref, left_ref, hot_ref
    )


def second_kernel(
    recv_ref, system_ref, vector_ref, image_ref, next_ref, slots_ref, edge_ref, weight_ref,
    out_ref, state_ref, turn_ref, few_ref, cams_ref, near_ref,
):
    near, back, curvature = exchange_in(
        recv_ref, slots_ref, edge_ref, weight_ref, turn_ref, few_ref, cams_ref, near_ref
    )
    degree = image_ref[6:7, :]
    alpha = image_ref[7:8, :] / curvature
    image_next = operator_rows(system_ref, next_ref, degree, near, back)
    sums = [jnp.zeros((1, 256), F32) for _ in range(3)]
    for a in range(6):
        at = LOOKUP[a, a]
        vector, image = vector_ref[a : a + 1, :], image_ref[a : a + 1, :]
        residual = -system_ref[21 + a : 22 + a, :] - alpha * image
        scaled = residual / (system_ref[at : at + 1, :] + DAMPING)
        scaled_image = image - alpha * image_next[a]
        sums[0] = sums[0] + residual * scaled
        sums[1] = sums[1] + scaled * scaled_image
        sums[2] = sums[2] + scaled * image + vector * scaled_image
        state_ref[a : a + 1, :] = residual
        state_ref[8 + a : 9 + a, :] = scaled
        state_ref[16 + a : 17 + a, :] = scaled_image
    state_ref[6:7, :] = alpha
    state_ref[7:8, :] = jnp.broadcast_to(curvature, (1, 256))
    lane = lax.broadcasted_iota(jnp.int32, (128, 128), 1)
    rows = [jnp.sum(value, axis=1, keepdims=True) for value in sums]
    out_ref[...] = jnp.where(lane == 0, rows[0], jnp.where(lane == 1, rows[1], rows[2]))


def last_kernel(recv_ref, vector_ref, image_ref, state_ref, step_ref, residual_ref):
    sums = jnp.sum(recv_ref[...], axis=0, keepdims=True)
    fresh, inner, cross = sums[:, 0:1], sums[:, 1:2], sums[:, 2:3]
    alpha, curvature = state_ref[6:7, 0:1], state_ref[7:8, 0:1]
    beta = fresh / image_ref[7:8, 0:1]
    alpha_next = fresh / (inner + beta * cross + beta * beta * curvature)
    vector, image = vector_ref[0:6, :], image_ref[0:6, :]
    direction = state_ref[8:14, :] + beta * vector
    step_ref[...] = alpha * vector + alpha_next * direction
    residual_ref[...] = state_ref[0:6, :] - alpha_next * (state_ref[16:22, :] + beta * image)


def kernels():
    vmem = pltpu.VMEM
    return {
        "poses": call(
            pose_kernel,
            "poses",
            array(1024, 128),
            [
                vmem((7, 256), F32),
                vmem((128, 128), jnp.int32),
                vmem((2, 128, 128), F32),
            ]
            + [pltpu.SemaphoreType.DMA] * 3,
            in_specs=[pl.BlockSpec(memory_space=pl.ANY)] * 3,
            vmem=None,
        ),
        "positions": call(position_kernel, "positions", array(3, 128, 128)),
        "eliminate": call(
            eliminate_kernel,
            "eliminate",
            array(1024, 128),
            [
                vmem((16, 72, 128), F32),
                vmem((12, 128, 128), F32),
                vmem((2, 288, 2048), BF16),
                vmem((16, 256, 1024), BF16),
                vmem((288, 256), F32),
                vmem((288, 128), F32),
                vmem((96, 128), F32),
                vmem((48, 256), F32),
                vmem((192, 256), BF16),
                vmem((2, 192, 2048), F32),
                vmem((2, 48, 128), F32),
            ],
        ),
        "cameras": call(
            camera_kernel,
            "cameras",
            (array(256, 128), array(32, 256), array(8, 256)),
            [
                vmem((2, 256, 128), F32),
                vmem((2, 64 * PARTS, 2048), BF16),
                vmem((2, 128, 2048), BF16),
                vmem((64 * PARTS, 128), F32),
            ]
            + OUT_SCRATCH,
        ),
        "first": call(
            first_kernel,
            "first_product",
            (array(256, 128), array(8, 256), array(8, 256)),
            OUT_SCRATCH + IN_SCRATCH,
        ),
        "second": call(
            second_kernel,
            "second_product",
            (array(128, 128), array(24, 256)),
            [OUT_SCRATCH[0]] + IN_SCRATCH,
        ),
        "last": call(last_kernel, "last", (array(6, 256), array(6, 256))),
    }


def swap(payload):
    blocks = payload.reshape(128, payload.shape[0] // 128, 128)
    return lax.all_to_all(blocks, AXES, split_axis=0, concat_axis=0, tiled=True).reshape(
        payload.shape
    )


def per_device(
    cam_pose, points, obs_uv, obs_cam, obs_pt, block_count, send_list, edge_slot, edge_weight
):
    run = kernels()
    cam_index = obs_cam.reshape(128, 128)
    point_index = obs_pt.reshape(128, 128)
    graph = (jnp.transpose(send_list.reshape(128, 16)), edge_slot, edge_weight)
    poses = run["poses"](cam_pose, cam_index, obs_uv.reshape(2, 128, 128))
    arrived = swap(poses)
    position = run["positions"](points, point_index)
    reduced = run["eliminate"](arrived, position, point_index, block_count)
    returned = swap(reduced)
    payload, system, vector = run["cameras"](returned, cam_index, *graph)
    payload, image, following = run["first"](swap(payload), system, vector, *graph)
    payload, state = run["second"](swap(payload), system, vector, image, following, *graph)
    return run["last"](swap(payload), vector, image, state)


def solution(mesh):
    in_specs = (
        P(None, AXES),
        P(None, AXES),
        P(None, AXES, None, None),
        P(AXES, None, None),
        P(AXES, None, None),
        P(AXES, None),
        P(AXES, None, None),
        P(None, AXES),
        P(None, AXES),
    )
    out_specs = (P(None, AXES), P(None, AXES))
    return jax.shard_map(
        per_device, mesh=mesh, in_specs=in_specs, out_specs=out_specs, check_vma=False
    )
```

```python
import functools

import jax
import jax.numpy as jnp
from jax import lax
from jax.experimental import pallas as pl
from jax.experimental.pallas import tpu as pltpu
from jax.sharding import PartitionSpec as P

AXES = ("gx", "gy")
DAMPING = 1.0
SYMMETRIC_PAIRS = [(a, b) for a in range(6) for b in range(a, 6)]
LOOKUP = {}
for _place, (_a, _b) in enumerate(SYMMETRIC_PAIRS):
    LOOKUP[_a, _b] = _place
    LOOKUP[_b, _a] = _place
POINT_PAIRS = [(0, 0), (0, 1), (0, 2), (1, 1), (1, 2), (2, 2)]
PARTS = 2

F32 = jnp.float32
BF16 = jnp.bfloat16


def call(
    kernel, name, out_shape, scratch=(), flops=1_000_000, bytes_accessed=1_000_000, vmem=48, **specs
):
    return pl.pallas_call(
        kernel,
        out_shape=out_shape,
        **specs,
        scratch_shapes=list(scratch),
        name=name,
        compiler_params=pltpu.CompilerParams(
            vmem_limit_bytes=vmem * 1024 * 1024 if vmem else None
        ),
        cost_estimate=pl.CostEstimate(
            flops=flops, bytes_accessed=bytes_accessed, transcendentals=0
        ),
    )


def array(*shape):
    return jax.ShapeDtypeStruct(shape, F32)


def eight(t):
    return t * 8 if isinstance(t, int) else pl.multiple_of(t * 8, 8)


def take(table, index):
    return jnp.take_along_axis(table, index, axis=1, mode="promise_in_bounds")


def spread(row, count):
    return jnp.broadcast_to(row, (count, row.shape[1]))


def parts_of(value):
    parts = []
    for _ in range(PARTS):
        part = value.astype(BF16).astype(F32)
        value = value - part
        parts.append(part)
    return parts


def dot_lanes(left, right):
    return lax.dot_general(left, right, (((1,), (1,)), ((), ())), preferred_element_type=F32)


def pose_kernel(
    pose_hbm, cam_hbm, uv_hbm, out_hbm, pose_ref, cam_ref, uv_ref, out_ref, pose_sem, cam_sem,
    uv_sem, out_sem,
):
    copies = [
        pltpu.make_async_copy(pose_hbm, pose_ref, pose_sem),
        pltpu.make_async_copy(cam_hbm, cam_ref, cam_sem),
        pltpu.make_async_copy(uv_hbm, uv_ref, uv_sem),
    ]
    for copy in copies:
        copy.start()
    for copy in copies[0:2]:
        copy.wait()
    inverse = 1.0 / pose_ref[0:1, :]
    pose_ref[1:4, :] = pose_ref[1:4, :] * inverse

    def tile(t):
        base = t * 8
        index = cam_ref[pl.ds(base, 8), :]
        lane, upper = index & 127, index >= 128
        for r in range(6):
            row = pose_ref[1 + r : 2 + r, :]
            out_ref[pl.ds(base * 8 + r, 8, stride=8), :] = jnp.where(
                upper,
                take(spread(row[:, 128:256], 8), lane),
                take(spread(row[:, 0:128], 8), lane),
            )
        for r in range(2):
            out_ref[pl.ds(base * 8 + 6 + r, 8, stride=8), :] = uv_ref[r, pl.ds(base, 8), :]

    def send(g):
        rows = pl.ds(g * 512, 512)
        return pltpu.make_async_copy(out_ref.at[rows], out_hbm.at[rows], out_sem.at[g])

    copies[2].wait()
    for g in range(2):
        for k in range(8):
            tile(8 * g + k)
        send(g).start()
    for g in range(2):
        send(g).wait()


def position_kernel(points_ref, index_ref, out_ref):
    def group(g, carry):
        base = pl.multiple_of(g * 32, 32)
        index = [index_ref[pl.ds(base + 8 * k, 8), :] for k in range(4)]
        lane = [value & 127 for value in index]
        chunk = [value >> 7 for value in index]
        found = [[jnp.zeros((8, 128), F32) for _ in range(4)] for _ in range(3)]
        for k in range(4):
            for h in range(32):
                for r in range(3):
                    row = spread(points_ref[r : r + 1, h * 128 : (h + 1) * 128], 8)
                    found[r][k] = jnp.where(chunk[k] == h, take(row, lane[k]), found[r][k])
        for r in range(3):
            for k in range(4):
                out_ref[r, pl.ds(base + 8 * k, 8), :] = found[r][k]
        return carry

    lax.fori_loop(0, 4, group, 0)


def onehot_rows(rows_ref, row, count, where, iota):
    value = spread(row, 16).astype(BF16)
    one, zero = jnp.ones((), BF16), jnp.zeros((), BF16)
    for q in range(count // 16):
        rows_ref[q * 16 : (q + 1) * 16, where : where + 128] = jnp.where(
            iota[q * 16 : (q + 1) * 16] == value, one, zero
        )


def iota_bf16(count):
    return lax.broadcasted_iota(jnp.int32, (count, 128), 0).astype(F32).astype(BF16)


def eliminate_kernel(
    recv_ref, position_ref, index_ref, count_ref, out_ref, term_ref, keep_ref, left_ref, hot_ref,
    sum_ref, half_ref, table_ref, rest_ref, parts_ref, picked_ref, found_ref,
):
    live_count = jnp.transpose(spread(count_ref[0:1, :], 128))
    keep_ref[11, :, :] = jnp.where(
        lax.broadcasted_iota(jnp.int32, (128, 128), 1) < live_count, 1.0, 0.0
    )

    def prepare(t, carry):
        base = pl.multiple_of(t * 8, 8)
        row = [recv_ref[pl.ds(base * 8 + r, 8, stride=8), :] for r in range(8)]
        x = [position_ref[r, pl.ds(base, 8), :] for r in range(3)]
        live = keep_ref[11, pl.ds(base, 8), :]
        q1, q2, q3 = row[0], row[1], row[2]
        s1, s2, s3 = q1 * q1, q2 * q2, q3 * q3
        scale = 1.0 / (1.0 + s1 + s2 + s3)
        q12, q13, q23 = q1 * q2, q1 * q3, q2 * q3
        rot = [
            (1.0 + s1 - s2 - s3) * scale,
            2.0 * (q12 - q3) * scale,
            2.0 * (q13 + q2) * scale,
            2.0 * (q12 + q3) * scale,
            (1.0 - s1 + s2 - s3) * scale,
            2.0 * (q23 - q1) * scale,
            2.0 * (q13 - q2) * scale,
            2.0 * (q23 + q1) * scale,
            (1.0 - s1 - s2 + s3) * scale,
        ]
        cam = [
            rot[3 * a] * x[0] + rot[3 * a + 1] * x[1] + rot[3 * a + 2] * x[2] + row[3 + a]
            for a in range(3)
        ]
        inverse = 1.0 / cam[2]
        u, v = cam[0] * inverse, cam[1] * inverse
        residue = [(u - row[6]) * live, (v - row[7]) * live]
        scaled = inverse * live
        jac = [
            [scaled * (rot[k] - u * rot[6 + k]) for k in range(3)],
            [scaled * (rot[3 + k] - v * rot[6 + k]) for k in range(3)],
        ]
        terms = [jac[0][k] * jac[0][l] + jac[1][k] * jac[1][l] for k, l in POINT_PAIRS]
        terms += [jac[0][k] * residue[0] + jac[1][k] * residue[1] for k in range(3)]
        for r in range(9):
            term_ref[t, 8 * r : 8 * r + 8, :] = terms[r]
        for r, value in enumerate(jac[0] + jac[1] + residue + [u, v, inverse]):
            keep_ref[r, pl.ds(base, 8), :] = value
        return carry

    lax.fori_loop(0, 16, prepare, 0, unroll=4)

    iota_chunk, iota_lane = iota_bf16(16), iota_bf16(256)
    zero = jnp.zeros((), BF16)

    def build(t, side, half):
        index = index_ref[pl.ds(pl.multiple_of(t * 8, 8), 8), :]
        lane, chunk = (index & 255).astype(F32), (index >> 8).astype(F32)
        for i in range(8):
            at = half * 1024 + i * 128
            onehot_rows(hot_ref.at[t], lane[i : i + 1, :], 256, i * 128, iota_lane)
            where = spread(chunk[i : i + 1, :], 16).astype(BF16)
            both = jnp.concatenate(parts_of(term_ref[t, pl.ds(i, 8, stride=8), :]), 0).astype(BF16)
            for h in range(16):
                left_ref[side, h * 16 : (h + 1) * 16, at : at + 128] = jnp.where(
                    where == h, both, zero
                )
            mask = iota_chunk == where
            for n, part in enumerate(parts_of(term_ref[t, 64 + i : 65 + i, :])):
                left_ref[side, 256 + 16 * n : 272 + 16 * n, at : at + 128] = jnp.where(
                    mask, spread(part, 16).astype(BF16), zero
                )

    def build_two(g, side):
        build(2 * g, side, 0)
        build(2 * g + 1, side, 1)

    def hot_two(g):
        return jnp.concatenate([hot_ref[2 * g], hot_ref[2 * g + 1]], 1)

    def product(g, side):
        sum_ref[...] += dot_lanes(left_ref[side], hot_two(g))

    sum_ref[...] = jnp.zeros_like(sum_ref)
    build_two(0, 0)

    def pair(p, carry):
        build_two(2 * p + 1, 1)
        product(2 * p, 0)
        build_two(2 * p + 2, 0)
        product(2 * p + 1, 1)
        return carry

    lax.fori_loop(0, 3, pair, 0)
    build_two(7, 1)
    product(6, 0)
    product(7, 1)

    for side in range(2):
        lanes = slice(side * 128, side * 128 + 128)
        half_ref[...] = sum_ref[:, lanes]
        sums = [
            half_ref[pl.ds(r, 16, stride=16), :] + half_ref[pl.ds(8 + r, 16, stride=16), :]
            for r in range(8)
        ] + [half_ref[256:272, :] + half_ref[272:288, :]]
        hess = [sums[0] + DAMPING, sums[1], sums[2], sums[3] + DAMPING, sums[4], sums[5] + DAMPING]
        cofactor = [
            hess[3] * hess[5] - hess[4] * hess[4],
            hess[2] * hess[4] - hess[1] * hess[5],
            hess[1] * hess[4] - hess[2] * hess[3],
            hess[0] * hess[5] - hess[2] * hess[2],
            hess[1] * hess[2] - hess[0] * hess[4],
            hess[0] * hess[3] - hess[1] * hess[1],
        ]
        determinant = hess[0] * cofactor[0] + hess[1] * cofactor[1] + hess[2] * cofactor[2]
        inv = [value / determinant for value in cofactor]
        grad = sums[6:9]
        solved = [
            inv[0] * grad[0] + inv[1] * grad[1] + inv[2] * grad[2],
            inv[1] * grad[0] + inv[3] * grad[1] + inv[4] * grad[2],
            inv[2] * grad[0] + inv[4] * grad[1] + inv[5] * grad[2],
        ]
        for r, value in enumerate(inv[0:4]):
            table_ref[pl.ds(r, 16, stride=4), :] = value
        for r, value in enumerate(inv[4:6]):
            table_ref[pl.ds(64 + r, 16, stride=2), :] = value
        for r, value in enumerate(solved):
            rest_ref[16 * r : 16 * r + 16, lanes] = value
        for h in range(12):
            parts_ref[h * 16 : (h + 1) * 16, lanes] = jnp.concatenate(
                parts_of(table_ref[8 * h : 8 * h + 8, :]), 0
            ).astype(BF16)

    def pick(g, side):
        picked_ref[side] = jnp.dot(parts_ref[...], hot_two(g), preferred_element_type=F32)

    def finish(t, side, half):
        base = eight(t)
        index = index_ref[pl.ds(base, 8), :]
        chunk = index >> 8

        def rows_of(first_row, count, where, at):
            parts = [jnp.zeros((8, 128), F32) for _ in range(PARTS)]
            for h in range(count):
                for n in range(PARTS):
                    row = first_row + 16 * h + 8 * n
                    parts[n] = jnp.where(
                        where == h, picked_ref[side, row : row + 8, at : at + 128], parts[n]
                    )
            return parts[0] + parts[1]

        for i in range(8):
            at = half * 1024 + i * 128
            where = spread(chunk[i : i + 1, :], 8)
            four = rows_of(0, 8, where >> 1, at)
            odd = spread(chunk[i : i + 1, :], 4) & 1
            found_ref[half, 4 * i : 4 * i + 4, :] = jnp.where(
                odd == 1, four[4:8, :], four[0:4, :]
            )
            two = rows_of(128, 4, where >> 2, at)
            step = spread(chunk[i : i + 1, :], 2) & 3
            found_ref[half, 32 + 2 * i : 34 + 2 * i, :] = jnp.where(
                step >= 2,
                jnp.where(step == 3, two[6:8, :], two[4:6, :]),
                jnp.where(step == 1, two[2:4, :], two[0:2, :]),
            )
        lane, chunk = index & 127, index >> 7
        rest = [jnp.zeros((8, 128), F32) for _ in range(3)]
        for h in range(32):
            for r in range(3):
                at = 16 * r + h // 2
                row = rest_ref[at : at + 1, (h % 2) * 128 : (h % 2) * 128 + 128]
                rest[r] = jnp.where(chunk == h, take(spread(row, 8), lane), rest[r])
        g0, g1, g2 = rest
        i0, i1, i2, i3 = [found_ref[half, pl.ds(r, 8, stride=4), :] for r in range(4)]
        i4, i5 = [found_ref[half, pl.ds(32 + r, 8, stride=2), :] for r in range(2)]
        kept = [keep_ref[r, pl.ds(base, 8), :] for r in range(12)]
        p, q = kept[0:3], kept[3:6]
        pv = [
            i0 * p[0] + i1 * p[1] + i2 * p[2],
            i1 * p[0] + i3 * p[1] + i4 * p[2],
            i2 * p[0] + i4 * p[1] + i5 * p[2],
        ]
        qv = [
            i0 * q[0] + i1 * q[1] + i2 * q[2],
            i1 * q[0] + i3 * q[1] + i4 * q[2],
            i2 * q[0] + i4 * q[1] + i5 * q[2],
        ]
        live = kept[11]
        values = [
            kept[8],
            kept[9],
            kept[10],
            live - (pv[0] * p[0] + pv[1] * p[1] + pv[2] * p[2]),
            -(pv[0] * q[0] + pv[1] * q[1] + pv[2] * q[2]),
            live - (qv[0] * q[0] + qv[1] * q[1] + qv[2] * q[2]),
            kept[6] - (p[0] * g0 + p[1] * g1 + p[2] * g2),
            kept[7] - (q[0] * g0 + q[1] * g1 + q[2] * g2),
        ]
        for r, value in enumerate(values):
            out_ref[pl.ds(base * 8 + r, 8, stride=8), :] = value

    def finish_two(g, side):
        finish(2 * g, side, 0)
        finish(2 * g + 1, side, 1)

    pick(0, 0)

    def pick_pair(p, carry):
        pick(2 * p + 1, 1)
        finish_two(2 * p, 0)
        pick(2 * p + 2, 0)
        finish_two(2 * p + 1, 1)
        return carry

    for p in range(3):
        pick_pair(p, 0)
    pick(7, 1)
    finish_two(6, 0)
    finish_two(7, 1)


def exchange_out(vector_ref, slots_ref, edge_ref, weight_ref, out_ref, turn_ref, left_ref, hot_ref):
    low, high = vector_ref[:, 0:128], vector_ref[:, 128:256]
    for j in range(16):
        index = spread(slots_ref[j : j + 1, :], 8)
        lane = index & 127
        turn_ref[8 * j : 8 * j + 8, :] = jnp.where(index >= 128, take(high, lane), take(low, lane))
    out_ref[pl.ds(0, 128, stride=2), :] = jnp.transpose(turn_ref[...])
    iota = iota_bf16(128)
    for k in range(8):
        for h in range(2):
            where = (2 * k + h) * 128
            edge = edge_ref[k : k + 1, h * 128 : (h + 1) * 128]
            onehot_rows(hot_ref, (edge >> 4).astype(F32), 128, where, iota)
            slot = spread(edge & 15, 8)
            weight = spread(weight_ref[k : k + 1, h * 128 : (h + 1) * 128], 8)
            for n, part in enumerate(parts_of(weight * (low, high)[h])):
                for j in range(0, 16, 2):
                    both = jnp.concatenate(
                        [jnp.where(slot == j, part, 0.0), jnp.where(slot == j + 1, part, 0.0)], 0
                    )
                    left_ref[n, 8 * j : 8 * j + 16, where : where + 128] = both.astype(BF16)
    summed = dot_lanes(hot_ref[...], left_ref[0])
    for n in range(1, PARTS):
        summed = summed + dot_lanes(hot_ref[...], left_ref[n])
    out_ref[pl.ds(1, 128, stride=2), :] = summed


def exchange_in(recv_ref, slots_ref, edge_ref, weight_ref, turn_ref, few_ref, cams_ref, near_ref):
    turn_ref[...] = jnp.transpose(recv_ref[pl.ds(0, 128, stride=2), :])
    for h in range(2):
        sums = jnp.zeros((8, 128), F32)
        for k in range(8):
            edge = edge_ref[k : k + 1, h * 128 : (h + 1) * 128]
            slot, peer = spread(edge & 15, 8), spread(edge >> 4, 8)
            near = jnp.zeros((8, 128), F32)
            for j in range(16):
                near = jnp.where(slot == j, take(turn_ref[8 * j : 8 * j + 8, :], peer), near)
            sums = sums + spread(weight_ref[k : k + 1, h * 128 : (h + 1) * 128], 8) * near
        near_ref[:, h * 128 : (h + 1) * 128] = sums
    scalar = jnp.sum(turn_ref[7:8, :], axis=1, keepdims=True)
    turn_ref[...] = jnp.transpose(recv_ref[pl.ds(1, 128, stride=2), :])
    iota = iota_bf16(256)
    for j in range(16):
        parts = parts_of(turn_ref[8 * j : 8 * j + 8, :])
        parts += [jnp.zeros((8, 128), F32)] * (4 - PARTS)
        few_ref[:, j * 128 : (j + 1) * 128] = jnp.concatenate(parts, 0).astype(BF16)
        onehot_rows(cams_ref, slots_ref[j : j + 1, :].astype(F32), 256, j * 128, iota)
    flow = dot_lanes(few_ref[...], cams_ref[...])
    back = flow[0:8, :]
    for n in range(1, PARTS):
        back = back + flow[8 * n : 8 * n + 8, :]
    return near_ref[...], back, scalar


OUT_SCRATCH = [
    pltpu.VMEM((128, 128), F32),
    pltpu.VMEM((PARTS, 128, 2048), BF16),
    pltpu.VMEM((128, 2048), BF16),
]
IN_SCRATCH = [
    pltpu.VMEM((32, 2048), BF16),
    pltpu.VMEM((256, 2048), BF16),
    pltpu.VMEM((8, 256), F32),
]


def block_product(system_ref, vector):
    return [
        sum(system_ref[LOOKUP[a, b] : LOOKUP[a, b] + 1, :] * vector[b] for b in range(6))
        for a in range(6)
    ]


def camera_kernel(
    recv_ref, index_ref, slots_ref, edge_ref, weight_ref, out_ref, system_ref, vector_ref,
    entry_ref, left_ref, hot_ref, sum_ref, turn_ref, edge_left_ref, edge_hot_ref,
):
    iota = iota_bf16(128)
    sum_ref[...] = jnp.zeros_like(sum_ref)
    entry_ref[:, 27 * 8 : 32 * 8, :] = jnp.zeros((2, 40, 128), F32)

    def build(t, side, half):
        base = pl.multiple_of(t * 8, 8)
        u, v, w, s00, s01, s11, f0, f1 = [
            recv_ref[pl.ds(base * 8 + r, 8, stride=8), :] for r in range(8)
        ]
        zero = jnp.zeros((8, 128), F32)
        uv = u * v
        top = [-uv, 1.0 + u * u, -v, w, zero, -u * w]
        low = [-1.0 - v * v, uv, u, zero, w, -v * w]
        g = [s00 * top[k] + s01 * low[k] for k in range(6)]
        h = [s01 * top[k] + s11 * low[k] for k in range(6)]
        for r, (a, b) in enumerate(SYMMETRIC_PAIRS):
            entry_ref[half, 8 * r : 8 * r + 8, :] = top[a] * g[b] + low[a] * h[b]
        for a in range(6):
            entry_ref[half, 8 * (21 + a) : 8 * (22 + a), :] = top[a] * f0 + low[a] * f1
        index = index_ref[pl.ds(base, 8), :]
        lane = (index & 127).astype(F32)
        for i in range(8):
            at = half * 1024 + i * 128
            onehot_rows(hot_ref.at[side], lane[i : i + 1, :], 128, at, iota)
            above = spread(index[i : i + 1, :], 32) >= 128
            for n, part in enumerate(parts_of(entry_ref[half, pl.ds(i, 32, stride=8), :])):
                left_ref[side, n * 32 : (n + 1) * 32, at : at + 128] = jnp.where(
                    above, 0.0, part
                ).astype(BF16)
                left_ref[side, 64 + n * 32 : 96 + n * 32, at : at + 128] = jnp.where(
                    above, part, 0.0
                ).astype(BF16)

    def build_two(g, side):
        build(2 * g, side, 0)
        build(2 * g + 1, side, 1)

    def product(side):
        sum_ref[...] += dot_lanes(left_ref[side], hot_ref[side])

    build_two(0, 0)

    def pair(p, carry):
        build_two(2 * p + 1, 1)
        product(0)
        build_two(2 * p + 2, 0)
        product(1)
        return carry

    lax.fori_loop(0, 3, pair, 0)
    build_two(7, 1)
    product(0)
    product(1)
    for h in range(2):
        at = 32 * PARTS * h
        system_ref[:, h * 128 : h * 128 + 128] = sum(
            sum_ref[at + 32 * n : at + 32 * n + 32, :] for n in range(PARTS)
        )
    partial = jnp.zeros((1, 256), F32)
    for a in range(6):
        at = LOOKUP[a, a]
        diagonal = system_ref[at : at + 1, :] + DAMPING
        residual = -system_ref[21 + a : 22 + a, :]
        scaled = residual / diagonal
        partial = partial + residual * scaled
        vector_ref[a : a + 1, :] = scaled
    vector_ref[6:7, :] = jnp.ones((1, 256), F32)
    vector_ref[7:8, :] = jnp.broadcast_to(jnp.sum(partial, axis=1, keepdims=True), (1, 256))
    exchange_out(
        vector_ref, slots_ref, edge_ref, weight_ref, out_ref, turn_ref, edge_left_ref, edge_hot_ref
    )


def operator_rows(system_ref, vector_ref, degree, near, back):
    vector = [vector_ref[a : a + 1, :] for a in range(6)]
    own = block_product(system_ref, vector)
    return [
        own[a] + (DAMPING + degree) * vector[a] - near[a : a + 1, :] - back[a : a + 1, :]
        for a in range(6)
    ]


def first_kernel(
    recv_ref, system_ref, vector_ref, slots_ref, edge_ref, weight_ref, out_ref, image_ref, next_ref,
    turn_ref, left_ref, hot_ref, few_ref, cams_ref, near_ref,
):
    near, back, scalar = exchange_in(
        recv_ref, slots_ref, edge_ref, weight_ref, turn_ref, few_ref, cams_ref, near_ref
    )
    degree = jnp.sum(weight_ref[...], axis=0, keepdims=True) + back[6:7, :]
    image = operator_rows(system_ref, vector_ref, degree, near, back)
    partial = jnp.zeros((1, 256), F32)
    for a in range(6):
        at = LOOKUP[a, a]
        partial = partial + vector_ref[a : a + 1, :] * image[a]
        image_ref[a : a + 1, :] = image[a]
        next_ref[a : a + 1, :] = image[a] / (system_ref[at : at + 1, :] + DAMPING)
    image_ref[6:7, :] = degree
    image_ref[7:8, :] = jnp.broadcast_to(scalar, (1, 256))
    next_ref[6:7, :] = jnp.ones((1, 256), F32)
    next_ref[7:8, :] = jnp.broadcast_to(jnp.sum(partial, axis=1, keepdims=True), (1, 256))
    exchange_out(
        next_ref, slots_ref, edge_ref, weight_ref, out_ref, turn_ref, left_ref, hot_ref
    )


def second_kernel(
    recv_ref, system_ref, vector_ref, image_ref, next_ref, slots_ref, edge_ref, weight_ref,
    out_ref, state_ref, turn_ref, few_ref, cams_ref, near_ref,
):
    near, back, curvature = exchange_in(
        recv_ref, slots_ref, edge_ref, weight_ref, turn_ref, few_ref, cams_ref, near_ref
    )
    degree = image_ref[6:7, :]
    alpha = image_ref[7:8, :] / curvature
    image_next = operator_rows(system_ref, next_ref, degree, near, back)
    sums = [jnp.zeros((1, 256), F32) for _ in range(3)]
    for a in range(6):
        at = LOOKUP[a, a]
        vector, image = vector_ref[a : a + 1, :], image_ref[a : a + 1, :]
        residual = -system_ref[21 + a : 22 + a, :] - alpha * image
        scaled = residual / (system_ref[at : at + 1, :] + DAMPING)
        scaled_image = image - alpha * image_next[a]
        sums[0] = sums[0] + residual * scaled
        sums[1] = sums[1] + scaled * scaled_image
        sums[2] = sums[2] + scaled * image + vector * scaled_image
        state_ref[a : a + 1, :] = residual
        state_ref[8 + a : 9 + a, :] = scaled
        state_ref[16 + a : 17 + a, :] = scaled_image
    state_ref[6:7, :] = alpha
    state_ref[7:8, :] = jnp.broadcast_to(curvature, (1, 256))
    lane = lax.broadcasted_iota(jnp.int32, (128, 128), 1)
    rows = [jnp.sum(value, axis=1, keepdims=True) for value in sums]
    out_ref[...] = jnp.where(lane == 0, rows[0], jnp.where(lane == 1, rows[1], rows[2]))


def last_kernel(recv_ref, vector_ref, image_ref, state_ref, step_ref, residual_ref):
    sums = jnp.sum(recv_ref[...], axis=0, keepdims=True)
    fresh, inner, cross = sums[:, 0:1], sums[:, 1:2], sums[:, 2:3]
    alpha, curvature = state_ref[6:7, 0:1], state_ref[7:8, 0:1]
    beta = fresh / image_ref[7:8, 0:1]
    alpha_next = fresh / (inner + beta * cross + beta * beta * curvature)
    vector, image = vector_ref[0:6, :], image_ref[0:6, :]
    direction = state_ref[8:14, :] + beta * vector
    step_ref[...] = alpha * vector + alpha_next * direction
    residual_ref[...] = state_ref[0:6, :] - alpha_next * (state_ref[16:22, :] + beta * image)


def kernels():
    vmem = pltpu.VMEM
    return {
        "poses": call(
            pose_kernel,
            "poses",
            array(1024, 128),
            [
                vmem((7, 256), F32),
                vmem((128, 128), jnp.int32),
                vmem((2, 128, 128), F32),
                vmem((1024, 128), F32),
            ]
            + [pltpu.SemaphoreType.DMA] * 3
            + [pltpu.SemaphoreType.DMA((2,))],
            in_specs=[pl.BlockSpec(memory_space=pl.ANY)] * 3,
            out_specs=pl.BlockSpec(memory_space=pl.ANY),
            vmem=None,
        ),
        "positions": call(position_kernel, "positions", array(3, 128, 128)),
        "eliminate": call(
            eliminate_kernel,
            "eliminate",
            array(1024, 128),
            [
                vmem((16, 72, 128), F32),
                vmem((12, 128, 128), F32),
                vmem((2, 288, 2048), BF16),
                vmem((16, 256, 1024), BF16),
                vmem((288, 256), F32),
                vmem((288, 128), F32),
                vmem((96, 128), F32),
                vmem((48, 256), F32),
                vmem((192, 256), BF16),
                vmem((2, 192, 2048), F32),
                vmem((2, 48, 128), F32),
            ],
        ),
        "cameras": call(
            camera_kernel,
            "cameras",
            (array(256, 128), array(32, 256), array(8, 256)),
            [
                vmem((2, 256, 128), F32),
                vmem((2, 64 * PARTS, 2048), BF16),
                vmem((2, 128, 2048), BF16),
                vmem((64 * PARTS, 128), F32),
            ]
            + OUT_SCRATCH,
        ),
        "first": call(
            first_kernel,
            "first_product",
            (array(256, 128), array(8, 256), array(8, 256)),
            OUT_SCRATCH + IN_SCRATCH,
        ),
        "second": call(
            second_kernel,
            "second_product",
            (array(128, 128), array(24, 256)),
            [OUT_SCRATCH[0]] + IN_SCRATCH,
        ),
        "last": call(last_kernel, "last", (array(6, 256), array(6, 256))),
    }


def swap(payload):
    blocks = payload.reshape(128, payload.shape[0] // 128, 128)
    return lax.all_to_all(blocks, AXES, split_axis=0, concat_axis=0, tiled=True).reshape(
        payload.shape
    )


def per_device(
    cam_pose, points, obs_uv, obs_cam, obs_pt, block_count, send_list, edge_slot, edge_weight
):
    run = kernels()
    cam_index = obs_cam.reshape(128, 128)
    point_index = obs_pt.reshape(128, 128)
    graph = (jnp.transpose(send_list.reshape(128, 16)), edge_slot, edge_weight)
    poses = run["poses"](cam_pose, cam_index, obs_uv.reshape(2, 128, 128))
    arrived = swap(poses)
    position = run["positions"](points, point_index)
    reduced = run["eliminate"](arrived, position, point_index, block_count)
    returned = swap(reduced)
    payload, system, vector = run["cameras"](returned, cam_index, *graph)
    payload, image, following = run["first"](swap(payload), system, vector, *graph)
    payload, state = run["second"](swap(payload), system, vector, image, following, *graph)
    return run["last"](swap(payload), vector, image, state)


def solution(mesh):
    in_specs = (
        P(None, AXES),
        P(None, AXES),
        P(None, AXES, None, None),
        P(AXES, None, None),
        P(AXES, None, None),
        P(AXES, None),
        P(AXES, None, None),
        P(None, AXES),
        P(None, AXES),
    )
    out_specs = (P(None, AXES), P(None, AXES))
    return jax.shard_map(
        per_device, mesh=mesh, in_specs=in_specs, out_specs=out_specs, check_vma=False
    )
```
